32 devices in a mesh: dp: 16 (over z, y, x), head: 2 (over core).
Axes of the slice: x: 2, y: 2, z: 4, core: 2. Of those that a mesh axis runs over, the one named last changes fastest.
Arguments:
- tokens: bfloat16 [32, 512, 768], P('dp'), may hold values from -6 to 6
- memory: bfloat16 [32, 20, 768], P('dp'), may hold values from -6 to 6
- query_weight: bfloat16 [768, 768], P(None, 'head'), may hold values from -0.21875 to 0.21875
- query_bias: bfloat16 [768], P('head'), may hold values from -3 to 3
- key_weight: bfloat16 [768, 768], P(None, 'head'), may hold values from -0.21875 to 0.21875
- value_weight: bfloat16 [768, 768], P(None, 'head'), may hold values from -0.21875 to 0.21875
- value_bias: bfloat16 [768], P('head'), may hold values from -3 to 3
- out_weight: bfloat16 [768, 768], P('head'), may hold values from -2.5 to 2.5
- out_bias: bfloat16 [768], replicated, may hold values from -3 to 3
- first_gain: bfloat16 [768], replicated, may hold values from 0.5 to 1.5
- first_shift: bfloat16 [768], replicated, may hold values from -3 to 3
- inner_weight: bfloat16 [768, 3072], P(None, 'head'), may hold values from -0.21875 to 0.21875
- inner_bias: bfloat16 [3072], P('head'), may hold values from -3 to 3
- outer_weight: bfloat16 [3072, 768], P('head'), may hold values from -0.109375 to 0.109375
- outer_bias: bfloat16 [768], replicated, may hold values from -3 to 3
- second_gain: bfloat16 [768], replicated, may hold values from 0.5 to 1.5
- second_shift: bfloat16 [768], replicated, may hold values from -3 to 3
- masked_rows: int32 [32, 80], P('dp'), may hold values from 0 to 511, as said below
- cotangent: bfloat16 [32, 80, 768], P('dp'), may hold values from -6 to 6
Outputs:
- layer_out: bfloat16 [32, 512, 768], P('dp', 'head')
- memory_out: bfloat16 [32, 20, 768], P('dp', 'head')
- tokens_grad: bfloat16 [32, 512, 768], P('dp', 'head')
- memory_grad: bfloat16 [32, 20, 768], P('dp', 'head')
- query_weight_grad: float32 [768, 768], P(None, 'head')
- query_bias_grad: float32 [768], P('head')
- key_weight_grad: float32 [768, 768], P(None, 'head')
- value_weight_grad: float32 [768, 768], P(None, 'head')
- value_bias_grad: float32 [768], P('head')
- out_weight_grad: float32 [768, 768], P('head')
- out_bias_grad: float32 [768], replicated
- first_gain_grad: float32 [768], replicated
- first_shift_grad: float32 [768], replicated
- inner_weight_grad: float32 [768, 3072], P(None, 'head')
- inner_bias_grad: float32 [3072], P('head')
- outer_weight_grad: float32 [3072, 768], P('head')
- outer_bias_grad: float32 [768], replicated
- second_gain_grad: float32 [768], replicated
- second_shift_grad: float32 [768], replicated
The draws below stay inside these ranges and needn't reach their ends.
Inputs may be any that keep to these rules, and one draw needn't show every extreme that they name: `masked_rows`: within each segment the 80 positions are distinct token positions.
All inputs are finite; a program needn't handle non-finite values.
Results may differ from the reference program's by a relative error of at most 0.019.
Values may be sent and summed in bfloat16 or wider, within the bound.
A program may use at most 192 MiB of HBM per device.

```python
import math
import jax
import jax.numpy as jnp
from jax import lax

D = 768
HEADS = 12
HDIM = 64
FF = 3072
SEQ = 512
MEM = 20
MASKED = 80
SEGS = 32


def draw_masked_rows(key, part):
    key = jax.random.fold_in(key, 11)
    seg_keys = jax.random.split(key, SEGS)

    def pick_rows(one_key):
        return jax.random.permutation(one_key, SEQ)[:MASKED]
    return jax.vmap(pick_rows)(seg_keys).astype(jnp.int32)


def block_scale(key, dims, cuts, smallest, top_value):
    gain = 1.0
    for position, shards_of in cuts:
        draws = jax.random.uniform(jax.random.fold_in(jax.random.fold_in(key, 6), position), (shards_of,), jnp.float32, smallest / len(cuts), top_value / len(cuts))
        gain = gain * jnp.repeat(jnp.exp(draws), dims[position] // shards_of).reshape((-1,) + (1,) * (len(dims) - 1 - position))
    return gain


def gaussian(stream_key, shape, width, bound, cuts=(), kind=jnp.bfloat16):
    values = jax.random.normal(stream_key, shape, jnp.float32) * width
    if len(cuts) > 0:
        values = block_scale(stream_key, shape, cuts, -0.22, 0.18) * values
    return jnp.clip(values, min=-bound, max=bound).astype(kind)


def setup_inputs(seed: int = 0) -> dict:
    splits = jax.random.split(jax.random.key(seed), 20)
    tokens = gaussian(splits[0], (SEGS, SEQ, D), 1.0, 6.0, ((0, 16),))
    memory = gaussian(splits[1], (SEGS, MEM, D), 1.0, 6.0, ((0, 16),))
    query_weight = gaussian(splits[2], (D, D), D ** -0.5, 0.21875, ((1, 2),))
    query_bias = gaussian(splits[3], (D,), 0.5, 3.0, ((0, 2),))
    key_weight = gaussian(splits[4], (D, D), D ** -0.5, 0.21875, ((1, 2),))
    value_weight = gaussian(splits[5], (D, D), D ** -0.5, 0.21875, ((1, 2),))
    value_bias = gaussian(splits[6], (D,), 0.5, 3.0, ((0, 2),))
    out_weight = gaussian(splits[7], (D, D), (max(D // 128, 1)) ** -0.5, 2.5, ((0, 2),))
    out_bias = gaussian(splits[8], (D,), 0.5, 3.0)
    first_gain = jnp.clip(1.0 + 0.1 * jax.random.normal(splits[9], (D,), jnp.float32), 0.5, 1.5).astype(jnp.bfloat16)
    first_shift = gaussian(splits[10], (D,), 0.5, 3.0)
    inner_weight = gaussian(splits[11], (D, FF), D ** -0.5, 0.21875, ((1, 2),))
    inner_bias = gaussian(splits[12], (FF,), 0.5, 3.0, ((0, 2),))
    outer_weight = gaussian(splits[13], (FF, D), FF ** -0.5, 0.109375, ((0, 2),))
    outer_bias = gaussian(splits[14], (D,), 0.5, 3.0)
    second_gain = jnp.clip(1.0 + 0.1 * jax.random.normal(splits[15], (D,), jnp.float32), 0.5, 1.5).astype(jnp.bfloat16)
    second_shift = gaussian(splits[16], (D,), 0.5, 3.0)
    masked_rows = draw_masked_rows(jax.random.fold_in(splits[19], 71), 0)
    cotangent = gaussian(splits[18], (SEGS, MASKED, D), 1.0, 6.0, ((0, 16),))
    return dict(tokens=tokens, memory=memory, query_weight=query_weight, query_bias=query_bias, key_weight=key_weight, value_weight=value_weight, value_bias=value_bias, out_weight=out_weight, out_bias=out_bias, first_gain=first_gain, first_shift=first_shift, inner_weight=inner_weight, inner_bias=inner_bias, outer_weight=outer_weight, outer_bias=outer_bias, second_gain=second_gain, second_shift=second_shift, masked_rows=masked_rows, cotangent=cotangent)


norm_eps = 1e-12

@jax.custom_vjp
def low(v):
    return lax.optimization_barrier(v.astype(jnp.bfloat16)).astype(jnp.float32)

@jax.custom_vjp
def low_back(v):
    return v

def low_keep(v):
    return (low(v), None)

def low_pass(kept, grad):
    return (grad,)

def back_keep(v):
    return (v, None)

def back_low(kept, grad):
    return (low(grad),)
low.defvjp(low_keep, low_pass)
low_back.defvjp(back_keep, back_low)

def norm_rows(values, gain_vector, shift_vector):
    center = values - lax.optimization_barrier(jnp.mean(values, axis=-1, keepdims=True))
    inverse = lax.rsqrt(lax.optimization_barrier(jnp.mean(center * center, axis=-1, keepdims=True)) + norm_eps)
    return center * inverse * gain_vector + shift_vector

def matmul(left, right):
    return jnp.dot(left, right, precision=lax.Precision.HIGHEST)

def segment_layer(param_set, memory_rows, token_rows):
    query_weight, query_bias, key_weight, value_weight, value_bias, out_weight, out_bias, first_gain, first_shift, inner_weight, inner_bias, outer_weight, outer_bias, second_gain, second_shift = param_set
    rows = jnp.concatenate([memory_rows, token_rows], axis=0)
    row_count = rows.shape[0]
    query_rows = low(low_back(matmul(rows, query_weight) + query_bias)).reshape(row_count, HEADS, HDIM)
    key_rows = low(low_back(matmul(rows, key_weight))).reshape(row_count, HEADS, HDIM)
    value_rows = low(low_back(matmul(rows, value_weight) + value_bias)).reshape(row_count, HEADS, HDIM)
    scores = low_back(jnp.einsum('qhd,khd->hqk', query_rows, key_rows, precision=lax.Precision.HIGHEST) / math.sqrt(HDIM))
    probs = jax.nn.softmax(scores, axis=-1)
    context = jnp.einsum('hqk,khd->qhd', low(probs), value_rows, precision=lax.Precision.HIGHEST)
    context = low(low_back(context.reshape(row_count, D)))
    attention = low_back(matmul(context, out_weight) + out_bias)
    normed = norm_rows(rows + attention, first_gain, first_shift)
    inner_act = low_back(matmul(low(normed), inner_weight) + inner_bias)
    activated = low(jax.nn.gelu(inner_act, approximate=False))
    outer = low_back(matmul(activated, outer_weight) + outer_bias)
    return norm_rows(normed + outer, second_gain, second_shift)

def group_layer(param_set, memory_set, token_set):
    return jax.vmap(segment_layer, in_axes=(None, 0, 0))(param_set, memory_set, token_set)

def add_pair(first_item, second_item):
    return first_item + second_item

def reference(tokens, memory, query_weight, query_bias, key_weight, value_weight, value_bias, out_weight, out_bias, first_gain, first_shift, inner_weight, inner_bias, outer_weight, outer_bias, second_gain, second_shift, masked_rows, cotangent):
    param_set = tuple((weight_item.astype(jnp.float32) for weight_item in (query_weight, query_bias, key_weight, value_weight, value_bias, out_weight, out_bias, first_gain, first_shift, inner_weight, inner_bias, outer_weight, outer_bias, second_gain, second_shift)))
    groups = SEGS // 4
    token_groups = tokens.astype(jnp.float32).reshape(groups, 4, SEQ, D)
    memory_groups = memory.astype(jnp.float32).reshape(groups, 4, MEM, D)
    index_groups = masked_rows.reshape(groups, 4, MASKED)
    cot_groups = cotangent.astype(jnp.float32).reshape(groups, 4, MASKED, D)

    def group_step(carry, batch):
        memory_set, token_set, index_set, cot_set = batch
        result, pull_back = jax.vjp(group_layer, param_set, memory_set, token_set)
        seg_index = jnp.arange(4, dtype=jnp.int32)[:, None]
        token_upstream = jnp.zeros((4, SEQ, D), jnp.float32).at[seg_index, index_set].add(cot_set)
        upstream = jnp.concatenate([jnp.zeros((4, MEM, D), jnp.float32), token_upstream], axis=1)
        param_grads, memory_grads, token_grads = pull_back(upstream)
        carry = jax.tree.map(add_pair, carry, param_grads)
        outputs = (result[:, MEM:].astype(jnp.bfloat16), result[:, :MEM].astype(jnp.bfloat16), token_grads.astype(jnp.bfloat16), memory_grads.astype(jnp.bfloat16))
        return (carry, outputs)
    zero_grads = tuple((jnp.zeros_like(weight_item) for weight_item in param_set))
    totals, stacked = lax.scan(group_step, zero_grads, (memory_groups, token_groups, index_groups, cot_groups))
    layer_out = stacked[0].reshape(SEGS, SEQ, D)
    memory_out = stacked[1].reshape(SEGS, MEM, D)
    tokens_grad = stacked[2].reshape(SEGS, SEQ, D)
    memory_grad = stacked[3].reshape(SEGS, MEM, D)
    return (layer_out, memory_out, tokens_grad, memory_grad, totals[0], totals[1], totals[2], totals[3], totals[4], totals[5], totals[6], totals[7], totals[8], totals[9], totals[10], totals[11], totals[12], totals[13], totals[14])
```

```python
import functools
import math

import jax
import jax.numpy as jnp
from jax import lax
from jax.experimental import pallas as pl
from jax.experimental.pallas import tpu as pltpu
from jax.sharding import PartitionSpec as P

HDIM = 64
GROUP = 16
MESH = pl.DeviceIdType.MESH

norm_eps = 1e-12
root_half = 1.0 / math.sqrt(2.0)
gauss_norm = 1.0 / math.sqrt(2.0 * math.pi)
low_type = jnp.bfloat16
full_type = jnp.float32


def norm_stats(values):
    center = values - jnp.mean(values, axis=-1, keepdims=True)
    inverse = lax.rsqrt(jnp.mean(center * center, axis=-1, keepdims=True) + norm_eps)
    return center * inverse, inverse


def norm_backward(upstream, scaled, inverse, gain_vector):
    weighted = upstream * gain_vector
    plain_mean = jnp.mean(weighted, axis=-1, keepdims=True)
    cross_mean = jnp.mean(weighted * scaled, axis=-1, keepdims=True)
    return inverse * (weighted - plain_mean - scaled * cross_mean)


def gelu_slope(pre_act):
    return (
        0.5 * (1.0 + lax.erf(pre_act * root_half))
        + pre_act * jnp.exp(-0.5 * pre_act * pre_act) * gauss_norm
    )


def product(form, left, right):
    return jnp.einsum(form, left, right, preferred_element_type=jnp.float32)


def row_sum(values):
    return jnp.sum(values, axis=(0, 1))


class Place:
    def __init__(self):
        index = lax.axis_index("dp")
        self.head = lax.axis_index("head")
        base = index // GROUP * GROUP
        inner = lax.rem(index, GROUP)
        self.x = lax.rem(inner, 2)
        self.y = lax.rem(inner // 2, 2)
        self.z = inner // 4
        self.base = base
        self.twin = (index, 1 - self.head)

    def at(self, x, y, z):
        return (self.base + z * 4 + y * 2 + x, self.head)

    def axes(self, flip):
        x_next = self.at(1 - self.x, self.y, self.z)
        y_next = self.at(self.x, 1 - self.y, self.z)
        if flip:
            return self.y, self.x, y_next, x_next
        return self.x, self.y, x_next, y_next

    def z_plus(self, step):
        return lax.rem(self.z + step, 4)

    def along_z(self, step):
        return self.at(self.x, self.y, self.z_plus(step))

    def partners(self):
        found = [self.twin, self.at(1 - self.x, self.y, self.z), self.at(self.x, 1 - self.y, self.z)]
        return found + [self.along_z(step) for step in (1, 2, 3)]


def meet(place):
    barrier = pltpu.get_barrier_semaphore()
    partners = place.partners()
    for partner in partners:
        pl.semaphore_signal(barrier, inc=1, device_id=partner, device_id_type=MESH)
    pl.semaphore_wait(barrier, len(partners))


def remote(src, dst, send, recv, device):
    return pltpu.make_async_remote_copy(
        src_ref=src, dst_ref=dst, send_sem=send, recv_sem=recv, device_id=device, device_id_type=MESH
    )


class Gather:
    def __init__(self, place, all_ref, half, send, recv, twin_send, twin_recv):
        self.place, self.all, self.half = place, all_ref, half
        self.send, self.recv, self.twin_send, self.twin_recv = send, recv, twin_send, twin_recv
        self.p, self.q, self.p_next, self.q_next = place.axes(half == 1)
        self.sends = []
        self.count = 0

    def block(self, q, p, z):
        return (q * 2 + p) * 4 + z

    def ref(self, block, kind):
        return self.all.at[kind, self.half, block]

    def pass_on(self, block, device):
        ref = self.ref(block, self.place.head)
        copy = remote(ref, ref, self.send.at[self.half, self.count], self.recv.at[self.half, block], device)
        copy.start()
        self.count += 1
        self.sends.append(copy)

    def to_twin(self, block):
        ref = self.ref(block, self.place.head)
        copy = remote(
            ref, ref, self.twin_send.at[self.half, block], self.twin_recv.at[self.half, block], self.place.twin
        )
        copy.start()

    def landed(self, block):
        ref = self.ref(block, self.place.head)
        remote(
            ref, ref, self.send.at[self.half, 0], self.recv.at[self.half, block], self.p_next
        ).wait_recv()

    def start(self):
        own = self.block(self.q, self.p, self.place.z)
        for step in (1, 3, 2):
            self.pass_on(own, self.place.along_z(step))
        self.pass_on(own, self.p_next)
        self.pass_on(own, self.q_next)
        self.to_twin(own)

    def z_step(self, step):
        block = self.block(self.q, self.p, self.place.z_plus(step))
        self.landed(block)
        self.pass_on(block, self.p_next)
        self.pass_on(block, self.q_next)
        self.to_twin(block)

    def p_step(self, step):
        block = self.block(self.q, 1 - self.p, self.place.z_plus(step))
        self.landed(block)
        self.pass_on(block, self.q_next)
        self.to_twin(block)

    def q_step(self, side, step):
        p = self.p if side == 0 else 1 - self.p
        block = self.block(1 - self.q, p, self.place.z_plus(step))
        self.landed(block)
        self.to_twin(block)

    def twin_landed(self, block):
        ref = self.ref(block, 1 - self.place.head)
        remote(
            ref, ref, self.twin_send.at[self.half, 0], self.twin_recv.at[self.half, block], self.place.twin
        ).wait_recv()

    def finish(self):
        for copy in self.sends:
            copy.wait_send()
        for block in range(GROUP):
            ref = self.ref(block, self.place.head)
            remote(
                ref, ref, self.twin_send.at[self.half, block], self.twin_recv.at[self.half, block], self.place.twin
            ).wait_send()


Z_ORDER = (0, 1, 3, 2)


class Reduce:
    def __init__(self, place, slot, src_ref, out_ref, first, second, third, acc, send, recv):
        self.place, self.slot = place, slot
        self.src, self.out = src_ref, out_ref
        self.first, self.second, self.third, self.acc = first, second, third, acc
        self.send, self.recv = send, recv
        self.p, self.q, self.p_next, self.q_next = place.axes(slot % 2 == 1)
        rows = src_ref.shape[0]
        self.p_rows, self.q_rows, self.z_rows = rows // 2, rows // 4, rows // 16
        self.count = 0
        self.copies = []

    def put(self, src, dst, device):
        copy = remote(src, dst, self.send.at[self.slot, self.count], self.recv.at[self.slot, self.count], device)
        copy.start()
        self.count += 1
        self.copies.append(copy)

    def landed(self, count):
        for copy in self.copies[-count:]:
            copy.wait_recv()

    def step_1(self):
        away = (1 - self.p) * self.p_rows
        self.put(self.src.at[pl.ds(away, self.p_rows)], self.first, self.p_next)

    def step_2(self):
        self.landed(1)
        kept = self.src[pl.ds(self.p * self.p_rows, self.p_rows)].astype(full_type)
        self.acc[...] = (kept + self.first[...].astype(full_type)).astype(low_type)
        away = (1 - self.q) * self.q_rows
        self.put(self.acc.at[pl.ds(away, self.q_rows)], self.second, self.q_next)

    def step_3(self):
        self.landed(1)
        mine = pl.ds(self.q * self.q_rows, self.q_rows)
        kept = self.acc[mine].astype(full_type)
        self.acc[mine] = (kept + self.second[...].astype(full_type)).astype(low_type)
        for step in (1, 3, 2):
            away = self.q * self.q_rows + self.place.z_plus(step) * self.z_rows
            self.put(self.acc.at[pl.ds(away, self.z_rows)], self.third.at[step - 1], self.place.along_z(step))

    def span(self):
        return self.p * self.p_rows + self.q * self.q_rows + self.place.z * self.z_rows

    def step_4(self):
        self.landed(3)
        total = self.acc[pl.ds(self.q * self.q_rows + self.place.z * self.z_rows, self.z_rows)].astype(full_type)
        for step in range(3):
            total += self.third[step].astype(full_type)
        mine = pl.ds(self.span(), self.z_rows)
        self.out[mine] = total.astype(low_type)
        for step in (1, 3, 2):
            self.put(self.out.at[mine], self.out.at[mine], self.place.along_z(step))

    def step_5(self):
        self.landed(3)
        mine = pl.ds(self.p * self.p_rows + self.q * self.q_rows, self.q_rows)
        self.put(self.out.at[mine], self.out.at[mine], self.q_next)

    def step_6(self):
        self.landed(1)
        mine = pl.ds(self.p * self.p_rows, self.p_rows)
        self.put(self.out.at[mine], self.out.at[mine], self.p_next)

    def finish(self):
        self.landed(1)
        for copy in self.copies:
            copy.wait_send()


class SmallGather:
    def __init__(self, place, all_ref, send, recv):
        self.place, self.all, self.send, self.recv = place, all_ref, send, recv
        self.line = (place.y * 2 + place.x) * 4
        self.copies = []

    def put(self, start, count, device):
        ref = self.all.at[pl.ds(start, count)]
        slot = len(self.copies)
        copy = remote(ref, ref, self.send.at[slot], self.recv.at[slot], device)
        copy.start()
        self.copies.append(copy)

    def step_1(self):
        for step in (1, 2, 3):
            self.put(self.line + self.place.z, 1, self.place.along_z(step))

    def step_2(self):
        for step in (1, 2, 3):
            ref = self.all.at[pl.ds(self.line + self.place.z_plus(step), 1)]
            remote(ref, ref, self.send.at[0], self.recv.at[3 - step], self.place.along_z(step)).wait_recv()
        self.put(self.line, 4, self.place.at(1 - self.place.x, self.place.y, self.place.z))

    def step_3(self):
        self.copies[3].wait_recv()
        self.put(self.place.y * 8, 8, self.place.at(self.place.x, 1 - self.place.y, self.place.z))

    def finish(self):
        self.copies[4].wait_recv()
        for copy in self.copies:
            copy.wait_send()


def transfer_kernel(
    factor_ref, grad_ref, small_ref,
    all_ref, sum_ref, small_all_ref,
    first, second, third, acc,
    g_send, g_recv, t_send, t_recv, r_send, r_recv, s_send, s_recv,
):
    place = Place()
    gathers = [Gather(place, all_ref, half, g_send, g_recv, t_send, t_recv) for half in range(2)]
    for half, gather in enumerate(gathers):
        own = gather.block(gather.q, gather.p, place.z)
        all_ref[place.head, half, own] = factor_ref[half]
    small = SmallGather(place, small_all_ref, s_send, s_recv)
    small_all_ref[small.line + place.z] = small_ref[...]
    reduces = [
        Reduce(
            place, slot, grad_ref.at[slot], sum_ref.at[slot], first.at[slot], second.at[slot], third.at[slot],
            acc.at[slot], r_send, r_recv,
        )
        for slot in range(4)
    ]
    meet(place)
    for gather in gathers:
        gather.start()
    for step in Z_ORDER[1:]:
        for gather in gathers:
            gather.z_step(step)
    for step in Z_ORDER:
        for gather in gathers:
            gather.p_step(step)
    small.step_1()
    reduces[0].step_1()
    reduces[1].step_1()
    for side in range(2):
        for step in Z_ORDER:
            for gather in gathers:
                gather.q_step(side, step)
    reduces[2].step_1()
    reduces[3].step_1()
    small.step_2()
    for name in ("step_2", "step_3", "step_4", "step_5", "step_6"):
        for pair in (0, 2):
            for reduce in reduces[pair : pair + 2]:
                getattr(reduce, name)()
        if name == "step_3":
            small.step_3()
    small.finish()
    for gather in gathers:
        for block in range(GROUP):
            gather.twin_landed(block)
    for reduce in reduces:
        reduce.finish()
    for gather in gathers:
        gather.finish()


def transfer(factor, grads, small):
    slots, rows, width = grads.shape
    vmem = pl.BlockSpec(memory_space=pltpu.VMEM)
    return pl.pallas_call(
        transfer_kernel,
        out_shape=(
            jax.ShapeDtypeStruct((2, 2, GROUP) + factor.shape[1:], low_type),
            jax.ShapeDtypeStruct(grads.shape, low_type),
            jax.ShapeDtypeStruct((GROUP,) + small.shape, full_type),
        ),
        in_specs=[vmem] * 3,
        out_specs=(vmem,) * 3,
        scratch_shapes=[
            pltpu.VMEM((slots, rows // 2, width), low_type),
            pltpu.VMEM((slots, rows // 4, width), low_type),
            pltpu.VMEM((slots, 3, rows // 16, width), low_type),
            pltpu.VMEM((slots, rows // 2, width), low_type),
            pltpu.SemaphoreType.DMA((2, 16)),
            pltpu.SemaphoreType.DMA((2, 16)),
            pltpu.SemaphoreType.DMA((2, 16)),
            pltpu.SemaphoreType.DMA((2, 16)),
            pltpu.SemaphoreType.DMA((slots, 10)),
            pltpu.SemaphoreType.DMA((slots, 10)),
            pltpu.SemaphoreType.DMA((5,)),
            pltpu.SemaphoreType.DMA((5,)),
        ],
        compiler_params=pltpu.CompilerParams(
            collective_id=0, has_side_effects=True, vmem_limit_bytes=48 * 2**20
        ),
    )(factor, grads, small)


def across_groups(values):
    size = lax.axis_size("dp")
    if size == GROUP:
        return values
    total = values
    moved = values
    for _ in range(size // GROUP - 1):
        moved = lax.ppermute(moved, "dp", [(i, (i + GROUP) % size) for i in range(size)])
        total = total + moved
    return total


def on_device(
    tokens,
    memory,
    query_weight,
    query_bias,
    key_weight,
    value_weight,
    value_bias,
    out_weight,
    out_bias,
    first_gain,
    first_shift,
    inner_weight,
    inner_bias,
    outer_weight,
    outer_bias,
    second_gain,
    second_shift,
    masked_rows,
    cotangent,
):
    seg_count, seq_len, feature_count = tokens.shape
    mem_len = memory.shape[1]
    all_rows = mem_len + seq_len
    masked = masked_rows.shape[1]
    local_heads = query_weight.shape[1] // HDIM
    score_scale = 1.0 / math.sqrt(HDIM)
    head = lax.axis_index("head")
    twin = lax.axis_size("head")

    def heads_view(values):
        return values.reshape(seg_count, values.shape[1], local_heads, HDIM)

    def flat_view(values):
        return values.reshape(seg_count, values.shape[1], local_heads * HDIM)

    def both(values):
        return lax.psum(values, "head")

    rows_low = jnp.concatenate([tokens, memory], axis=1)
    key_low = product("srd,de->sre", rows_low, key_weight).astype(low_type)
    value_low = (product("srd,de->sre", rows_low, value_weight) + value_bias).astype(low_type)
    key_heads = heads_view(key_low)
    value_heads = heads_view(value_low)

    pick = (masked_rows[:, :, None] == jnp.arange(seq_len, dtype=jnp.int32)).astype(low_type)
    rows_m = product("smt,std->smd", pick, tokens).astype(low_type)
    query_m = heads_view((product("smd,de->sme", rows_m, query_weight) + query_bias).astype(low_type))
    scores_m = product("smhd,skhd->shmk", query_m, key_heads) * score_scale
    probs_m = jax.nn.softmax(scores_m, axis=-1)
    probs_m_low = probs_m.astype(low_type)
    context_m = flat_view(product("shmk,skhd->smhd", probs_m_low, value_heads)).astype(low_type)
    attention_m = both(product("sme,ed->smd", context_m, out_weight)) + out_bias
    first_scaled, first_inverse = norm_stats(rows_m.astype(full_type) + attention_m)
    normed_m = first_scaled * first_gain + first_shift
    normed_m_low = normed_m.astype(low_type)
    inner_m = product("smd,df->smf", normed_m_low, inner_weight) + inner_bias
    active_m = jax.nn.gelu(inner_m, approximate=False).astype(low_type)
    outer_m = both(product("smf,fd->smd", active_m, outer_weight)) + outer_bias
    second_scaled, second_inverse = norm_stats(normed_m + outer_m)
    upstream = cotangent.astype(full_type)
    second_in_grad = norm_backward(upstream, second_scaled, second_inverse, second_gain.astype(full_type))
    outer_grad = second_in_grad.astype(low_type)
    inner_grad = (product("smd,fd->smf", outer_grad, outer_weight) * gelu_slope(inner_m)).astype(low_type)
    normed_grad = second_in_grad + both(product("smf,df->smd", inner_grad, inner_weight))
    first_in_grad = norm_backward(normed_grad, first_scaled, first_inverse, first_gain.astype(full_type))
    attention_grad = first_in_grad.astype(low_type)
    out_weight_grad = product("sme,smd->ed", context_m, attention_grad)
    context_grad = heads_view(product("smd,ed->sme", attention_grad, out_weight).astype(low_type))
    probs_grad = product("smhd,skhd->shmk", context_grad, value_heads)
    score_grad = (
        probs_m * (probs_grad - jnp.sum(probs_m * probs_grad, axis=-1, keepdims=True))
    ).astype(low_type)
    value_grad = flat_view(product("shmk,smhd->skhd", probs_m_low, context_grad)).astype(low_type)
    query_grad = flat_view(product("shmk,skhd->smhd", score_grad, key_heads) * score_scale).astype(low_type)
    key_grad = flat_view(product("shmk,smhd->skhd", score_grad, query_m) * score_scale).astype(low_type)
    query_weight_grad = product("smd,sme->de", rows_m, query_grad)
    key_weight_grad = product("srd,sre->de", rows_low, key_grad)
    value_weight_grad = product("srd,sre->de", rows_low, value_grad)

    small = jnp.stack(
        [
            row_sum(attention_grad.astype(full_type)),
            row_sum(normed_grad * first_scaled),
            row_sum(normed_grad),
            row_sum(upstream * second_scaled),
            row_sum(upstream),
            jnp.concatenate(
                [row_sum(query_grad.astype(full_type)), row_sum(value_grad.astype(full_type))]
            ),
            jnp.zeros((feature_count,), full_type),
            jnp.zeros((feature_count,), full_type),
        ]
    )

    input_part = product("sre,de->srd", key_grad, key_weight)
    input_part = input_part + product("sre,de->srd", value_grad, value_weight)
    masked_part = product("sme,de->smd", query_grad, query_weight) + jnp.where(head == 0, first_in_grad, 0.0)
    masked_high = masked_part.astype(low_type)
    masked_rest = (masked_part - masked_high.astype(full_type)).astype(low_type)
    spread = product("smt,smd->std", pick, masked_high) + product("smt,smd->std", pick, masked_rest)

    def exchange(values):
        return lax.psum_scatter(values.astype(low_type), "head", scatter_dimension=1, tiled=True)

    tokens_grad = exchange(input_part[:, :seq_len] + spread)
    memory_grad = exchange(input_part[:, seq_len:])

    query_heads = heads_view((product("srd,de->sre", rows_low, query_weight) + query_bias).astype(low_type))
    scores = product("sqhd,skhd->shqk", query_heads, key_heads) * score_scale
    raised = jnp.exp(scores - jnp.max(scores, axis=-1, keepdims=True))
    total = jnp.sum(raised, axis=-1, keepdims=True)
    context = product("shqk,skhd->shqd", raised.astype(low_type), value_heads) / total
    context = flat_view(jnp.swapaxes(context, 1, 2)).astype(low_type)
    attention_part = product("sre,ed->srd", context, out_weight)
    attention = jnp.concatenate(
        [exchange(attention_part[:, :seq_len]), exchange(attention_part[:, seq_len:])], axis=1
    ).astype(full_type)
    own_seq, own_mem = seq_len // twin, mem_len // twin
    rows_own = jnp.concatenate(
        [
            lax.dynamic_slice_in_dim(tokens, head * own_seq, own_seq, 1),
            lax.dynamic_slice_in_dim(memory, head * own_mem, own_mem, 1),
        ],
        axis=1,
    ).astype(full_type)
    scaled, _ = norm_stats(rows_own + attention + out_bias)
    normed = scaled * first_gain + first_shift
    normed_low = lax.all_gather(normed.astype(low_type), "head", axis=0, tiled=False)
    normed_low = jnp.concatenate(
        [normed_low[i, :, :own_seq] for i in range(twin)] + [normed_low[i, :, own_seq:] for i in range(twin)], axis=1
    )
    inner_act = product("srd,df->srf", normed_low, inner_weight) + inner_bias
    activated = jax.nn.gelu(inner_act, approximate=False).astype(low_type)
    outer_part = product("srf,fd->srd", activated, outer_weight)
    outer = jnp.concatenate(
        [exchange(outer_part[:, :seq_len]), exchange(outer_part[:, seq_len:])], axis=1
    ).astype(full_type)
    scaled, _ = norm_stats(normed + outer + outer_bias)
    result = (scaled * second_gain + second_shift).astype(low_type)
    layer_out, memory_out = result[:, :own_seq], result[:, own_seq:]

    factor = jnp.where(head == 0, normed_m_low, outer_grad)
    half = out_weight.shape[0]
    grads = jnp.stack(
        [
            jnp.concatenate([out_weight_grad[:, :half], out_weight_grad[:, half:]], axis=0),
            query_weight_grad,
            key_weight_grad,
            value_weight_grad,
        ]
    ).astype(low_type)
    factors, sums, smalls = transfer(factor, grads, small)
    normed_all = factors[0].reshape(-1, feature_count)
    outer_all = factors[1].reshape(-1, feature_count)
    inner_all = product("md,df->mf", normed_all, inner_weight) + inner_bias
    active_all = jax.nn.gelu(inner_all, approximate=False).astype(low_type)
    inner_grad_all = (product("md,fd->mf", outer_all, outer_weight) * gelu_slope(inner_all)).astype(low_type)
    outer_weight_grad = across_groups(product("mf,md->fd", active_all, outer_all))
    inner_weight_grad = across_groups(product("md,mf->df", normed_all, inner_grad_all))
    inner_bias_grad = across_groups(jnp.sum(inner_grad_all.astype(full_type), axis=0))
    outer_bias_grad = across_groups(jnp.sum(outer_all.astype(full_type), axis=0))
    sums = across_groups(sums.astype(full_type))
    smalls = across_groups(jnp.sum(smalls, axis=0))
    return (
        layer_out,
        memory_out,
        tokens_grad,
        memory_grad,
        sums[1],
        smalls[5, :half],
        sums[2],
        sums[3],
        smalls[5, half:],
        jnp.concatenate([sums[0, :half], sums[0, half:]], axis=1),
        smalls[0],
        smalls[1],
        smalls[2],
        inner_weight_grad,
        inner_bias_grad,
        outer_weight_grad,
        outer_bias_grad,
        smalls[3],
        smalls[4],
    )


def solution(mesh):
    return jax.shard_map(
        on_device,
        mesh=mesh,
        in_specs=(
            P("dp", None, None),
            P("dp", None, None),
            P(None, "head"),
            P("head"),
            P(None, "head"),
            P(None, "head"),
            P("head"),
            P("head", None),
            P(),
            P(),
            P(),
            P(None, "head"),
            P("head"),
            P("head", None),
            P(),
            P(),
            P(),
            P("dp", None),
            P("dp", None, None),
        ),
        out_specs=(
            P("dp", "head", None),
            P("dp", "head", None),
            P("dp", "head", None),
            P("dp", "head", None),
            P(None, "head"),
            P("head"),
            P(None, "head"),
            P(None, "head"),
            P("head"),
            P("head", None),
            P(),
            P(),
            P(),
            P(None, "head"),
            P("head"),
            P("head", None),
            P(),
            P(),
            P(),
        ),
        check_vma=False,
    )
```

```python
import math

import jax
import jax.numpy as jnp
from jax import lax
from jax.experimental import pallas as pl
from jax.experimental.pallas import tpu as pltpu
from jax.sharding import PartitionSpec as P

HDIM = 64
GROUP = 16
MESH = pl.DeviceIdType.MESH

norm_eps = 1e-12
root_half = 1.0 / math.sqrt(2.0)
gauss_norm = 1.0 / math.sqrt(2.0 * math.pi)
low_type = jnp.bfloat16
full_type = jnp.float32


def norm_stats(values):
    center = values - jnp.mean(values, axis=-1, keepdims=True)
    inverse = lax.rsqrt(jnp.mean(center * center, axis=-1, keepdims=True) + norm_eps)
    return center * inverse, inverse


def norm_backward(upstream, scaled, inverse, gain_vector):
    weighted = upstream * gain_vector
    plain_mean = jnp.mean(weighted, axis=-1, keepdims=True)
    cross_mean = jnp.mean(weighted * scaled, axis=-1, keepdims=True)
    return inverse * (weighted - plain_mean - scaled * cross_mean)


class Place:
    def __init__(self):
        index = lax.axis_index("dp")
        self.head = lax.axis_index("head")
        base = index // GROUP * GROUP
        inner = lax.rem(index, GROUP)
        self.x = lax.rem(inner, 2)
        self.y = lax.rem(inner // 2, 2)
        self.z = inner // 4
        self.base = base
        self.twin = (index, 1 - self.head)

    def at(self, x, y, z):
        return (self.base + z * 4 + y * 2 + x, self.head)

    def axes(self, flip):
        x_next = self.at(1 - self.x, self.y, self.z)
        y_next = self.at(self.x, 1 - self.y, self.z)
        if flip:
            return self.y, self.x, y_next, x_next
        return self.x, self.y, x_next, y_next

    def z_plus(self, step):
        return lax.rem(self.z + step, 4)

    def along_z(self, step):
        return self.at(self.x, self.y, self.z_plus(step))

    def partners(self):
        found = [self.twin, self.at(1 - self.x, self.y, self.z), self.at(self.x, 1 - self.y, self.z)]
        return found + [self.along_z(step) for step in (1, 2, 3)]


def remote(src, dst, send, recv, device):
    return pltpu.make_async_remote_copy(
        src_ref=src, dst_ref=dst, send_sem=send, recv_sem=recv, device_id=device, device_id_type=MESH
    )


Z_ORDER = (0, 1, 3, 2)


class Reduce:
    def __init__(self, place, slot, src_ref, out_ref, first, second, third, acc, send, recv):
        self.place, self.slot = place, slot
        self.src, self.out = src_ref, out_ref
        self.first, self.second, self.third, self.acc = first, second, third, acc
        self.send, self.recv = send, recv
        self.p, self.q, self.p_next, self.q_next = place.axes(slot % 2 == 1)
        rows = src_ref.shape[0]
        self.p_rows, self.q_rows, self.z_rows = rows // 2, rows // 4, rows // 16
        self.count = 0
        self.copies = []

    def put(self, src, dst, device):
        copy = remote(src, dst, self.send.at[self.slot, self.count], self.recv.at[self.slot, self.count], device)
        copy.start()
        self.count += 1
        self.copies.append(copy)

    def landed(self, count):
        for copy in self.copies[-count:]:
            copy.wait_recv()

    def step_1(self):
        away = (1 - self.p) * self.p_rows
        self.put(self.src.at[pl.ds(away, self.p_rows)], self.first, self.p_next)

    def step_2(self):
        self.landed(1)
        kept = self.src[pl.ds(self.p * self.p_rows, self.p_rows)].astype(full_type)
        self.acc[...] = (kept + self.first[...].astype(full_type)).astype(low_type)
        away = (1 - self.q) * self.q_rows
        self.put(self.acc.at[pl.ds(away, self.q_rows)], self.second, self.q_next)

    def step_3(self):
        self.landed(1)
        mine = pl.ds(self.q * self.q_rows, self.q_rows)
        kept = self.acc[mine].astype(full_type)
        self.acc[mine] = (kept + self.second[...].astype(full_type)).astype(low_type)
        for step in (1, 3, 2):
            away = self.q * self.q_rows + self.place.z_plus(step) * self.z_rows
            self.put(self.acc.at[pl.ds(away, self.z_rows)], self.third.at[step - 1], self.place.along_z(step))

    def span(self):
        return self.p * self.p_rows + self.q * self.q_rows + self.place.z * self.z_rows

    def step_4(self):
        self.landed(3)
        total = self.acc[pl.ds(self.q * self.q_rows + self.place.z * self.z_rows, self.z_rows)].astype(full_type)
        for step in range(3):
            total += self.third[step].astype(full_type)
        mine = pl.ds(self.span(), self.z_rows)
        self.out[mine] = total.astype(low_type)
        for step in (1, 3, 2):
            self.put(self.out.at[mine], self.out.at[mine], self.place.along_z(step))

    def step_5(self):
        self.landed(3)
        mine = pl.ds(self.p * self.p_rows + self.q * self.q_rows, self.q_rows)
        self.put(self.out.at[mine], self.out.at[mine], self.q_next)

    def step_6(self):
        self.landed(1)
        mine = pl.ds(self.p * self.p_rows, self.p_rows)
        self.put(self.out.at[mine], self.out.at[mine], self.p_next)

    def finish(self):
        self.landed(1)
        for copy in self.copies:
            copy.wait_send()


class SmallGather:
    def __init__(self, place, all_ref, send, recv):
        self.place, self.all, self.send, self.recv = place, all_ref, send, recv
        self.line = (place.y * 2 + place.x) * 4
        self.copies = []

    def put(self, start, count, device):
        ref = self.all.at[pl.ds(start, count)]
        slot = len(self.copies)
        copy = remote(ref, ref, self.send.at[slot], self.recv.at[slot], device)
        copy.start()
        self.copies.append(copy)

    def step_1(self):
        for step in (1, 2, 3):
            self.put(self.line + self.place.z, 1, self.place.along_z(step))

    def step_2(self):
        for step in (1, 2, 3):
            ref = self.all.at[pl.ds(self.line + self.place.z_plus(step), 1)]
            remote(ref, ref, self.send.at[0], self.recv.at[3 - step], self.place.along_z(step)).wait_recv()
        self.put(self.line, 4, self.place.at(1 - self.place.x, self.place.y, self.place.z))

    def step_3(self):
        self.copies[3].wait_recv()
        self.put(self.place.y * 8, 8, self.place.at(self.place.x, 1 - self.place.y, self.place.z))

    def finish(self):
        self.copies[4].wait_recv()
        for copy in self.copies:
            copy.wait_send()


def dots(left, right, left_dim=1, right_dim=0):
    return lax.dot_general(
        left, right, (((left_dim,), (right_dim,)), ((), ())), preferred_element_type=full_type
    )


def at_rows(start, count):
    return pl.ds(pl.multiple_of(start, 16), count)


def lanes(index, count):
    return pl.ds(pl.multiple_of(index * count, count), count)


def repeat(count, body):
    def step(index, carry):
        body(index)
        return carry

    lax.fori_loop(0, count, step, 0)


class Gather:
    def __init__(self, place, all_ref, half, send, recv, twin_send, twin_recv):
        self.place, self.all, self.half = place, all_ref, half
        self.size = all_ref.shape[1] // (2 * GROUP)
        self.send, self.recv, self.twin_send, self.twin_recv = send, recv, twin_send, twin_recv
        self.p, self.q, self.p_next, self.q_next = place.axes(half == 1)
        self.own = self.block(self.q, self.p, place.z)
        self.sends = []
        self.twins = []

    def block(self, q, p, z):
        return (q * 2 + p) * 4 + z

    def rows(self, block):
        return at_rows((self.half * GROUP + block) * self.size, self.size)

    def ref(self, block, kind):
        return self.all.at[kind, self.rows(block)]

    def pass_on(self, block, device):
        ref = self.ref(block, self.place.head)
        copy = remote(ref, ref, self.send.at[self.half, len(self.sends)], self.recv.at[self.half, block], device)
        copy.start()
        self.sends.append(copy)

    def to_twin(self, block):
        ref = self.ref(block, self.place.head)
        slot = self.twin_send.at[self.half, len(self.twins)]
        copy = remote(ref, ref, slot, self.twin_recv.at[self.half, block], self.place.twin)
        copy.start()
        self.twins.append(copy)

    def landed(self, block):
        ref = self.ref(block, self.place.head)
        remote(ref, ref, self.send.at[self.half, 0], self.recv.at[self.half, block], self.p_next).wait_recv()

    def start(self):
        for step in (1, 3, 2):
            self.pass_on(self.own, self.place.along_z(step))
        self.pass_on(self.own, self.p_next)
        self.pass_on(self.own, self.q_next)

    def z_step(self, step):
        block = self.block(self.q, self.p, self.place.z_plus(step))
        self.landed(block)
        self.pass_on(block, self.p_next)
        self.pass_on(block, self.q_next)
        self.to_twin(block)

    def p_step(self, step):
        block = self.block(self.q, 1 - self.p, self.place.z_plus(step))
        self.landed(block)
        self.pass_on(block, self.q_next)
        self.to_twin(block)

    def q_step(self, side, step):
        p = self.p if side == 0 else 1 - self.p
        block = self.block(1 - self.q, p, self.place.z_plus(step))
        self.landed(block)
        self.to_twin(block)

    def all_landed(self):
        kind = 1 - self.place.head
        for side in range(2):
            for other in range(2):
                for step in Z_ORDER:
                    if side + other + step == 0:
                        continue
                    q = self.q if side == 0 else 1 - self.q
                    p = self.p if other == 0 else 1 - self.p
                    block = self.block(q, p, self.place.z_plus(step))
                    ref = self.ref(block, kind)
                    remote(
                        ref, ref, self.twin_send.at[self.half, 0], self.twin_recv.at[self.half, block], self.place.twin
                    ).wait_recv()

    def finish(self):
        for copy in self.sends + self.twins:
            copy.wait_send()


def layer_kernel(
    tokens_any, memory_any, query_any, key_any, value_any, out_any, inner_any, outer_any,
    index_ref, cot_ref, vec_ref,
    layer_out_ref, memory_out_ref, tokens_grad_ref, memory_grad_ref, sum_ref, outer_grad_ref, inner_grad_ref,
    vec_out_ref,
    rows, wq, wkv, wo, wi, wu, load_sem,
    pick, keys, values, pair_values, rows_m, query_m, probs, context_m, swap_out, swap_in,
    first_scaled, fig, slope, query_grad, kv_grad, spread, stage,
    all_ref, small_all, grads, first, second, third, acc,
    part_t, got_t, query_d, context_d, normed_d, pool,
    g_send, g_recv, t_send, t_recv, r_send, r_recv, s_send, s_recv, x_send, x_recv,
):
    segs, seq, width = tokens_any.shape
    mem_pad = memory_any.shape[1]
    tall = seq + mem_pad
    masked = cot_ref.shape[1]
    m_rows = segs * masked
    own_seq = seq // 2
    own = own_seq + mem_pad
    half = query_any.shape[1]
    pairs = half // 128
    key_rows = keys.shape[1]
    mem_len = key_rows
    hidden = inner_any.shape[1]
    place = Place()
    head = place.head
    gate = lax.broadcasted_iota(jnp.int32, (1, 128), 1) < HDIM
    score_scale = 1.0 / math.sqrt(HDIM)

    loads = []

    def load(src, dst):
        copy = pltpu.make_async_copy(src, dst, load_sem.at[len(loads)])
        copy.start()
        loads.append(copy)
        return copy

    load_rows = []
    for s in range(segs):
        load_rows.append(load(tokens_any.at[s], rows.at[pl.ds(s * tall, seq)]))
        load_rows.append(load(memory_any.at[s], rows.at[pl.ds(s * tall + seq, mem_pad)]))
    load_kv = [load(key_any, wkv.at[:, pl.ds(0, half)]), load(value_any, wkv.at[:, pl.ds(half, half)])]
    load_q, load_o = load(query_any, wq), load(out_any, wo)
    load_i, load_u = load(inner_any, wi), load(outer_any, wu)

    barrier = pltpu.get_barrier_semaphore()
    partners = place.partners()
    for partner in partners:
        pl.semaphore_signal(barrier, inc=1, device_id=partner, device_id_type=MESH)

    out_bias, first_gain, first_shift = vec_ref[0:1], vec_ref[1:2], vec_ref[2:3]
    outer_bias, second_gain, second_shift = vec_ref[3:4], vec_ref[4:5], vec_ref[5:6]
    query_bias, value_bias = vec_ref[6:7, :half], vec_ref[6:7, half:]
    key_mask = vec_ref[10:11, : key_rows - seq]

    def inner_bias(part):
        return vec_ref[8 + part : 9 + part]

    keys[:, pl.ds(tall, key_rows - tall)] = jnp.zeros((segs, key_rows - tall, half), low_type)
    values[:, pl.ds(tall, key_rows - tall)] = jnp.zeros((segs, key_rows - tall, half), low_type)
    for s in range(segs):
        index = index_ref[s]
        hot = jnp.where(index == lax.broadcasted_iota(jnp.int32, (masked, seq), 1), 1.0, 0.0).astype(low_type)
        pick[s, 0:masked] = hot
        pick[s, masked : 2 * masked] = hot

    for copy in load_rows + load_kv:
        copy.wait()

    def key_value(s):
        both = dots(rows[at_rows(s * tall, tall)], wkv[...])
        keys[s, 0:tall] = both[:, :half].astype(low_type)
        values[s, 0:tall] = (both[:, half:] + value_bias).astype(low_type)

    repeat(segs, key_value)

    load_q.wait()
    for s in range(segs):
        m = pl.ds(s * masked, masked)
        found = dots(pick[s, 0:masked], rows[pl.ds(s * tall, seq)]).astype(low_type)
        rows_m[m] = found
    query_m[...] = (dots(rows_m[...], wq[...]) + query_bias).astype(low_type)

    def apart(pair):
        zero = jnp.zeros_like(pair)
        return jnp.concatenate([jnp.where(gate, pair, zero), jnp.where(gate, zero, pair)], axis=0)

    def masked_attention(i):
        s, pair = i // pairs, lax.rem(i, pairs)
        m, cols = at_rows(s * masked, masked), lanes(pair, 128)
        scores = dots(apart(query_m[m, cols]), keys[s, :, cols], 1, 1) * score_scale
        scores = jnp.concatenate([scores[:, :seq], scores[:, seq:] + key_mask], axis=1)
        raised = jnp.exp(scores - jnp.max(scores, axis=1, keepdims=True))
        share = raised / jnp.sum(raised, axis=1, keepdims=True)
        probs[i] = share
        found = dots(share.astype(low_type), values[s, :, cols])
        context_m[m, cols] = jnp.where(gate, found[:masked], found[masked:]).astype(low_type)

    repeat(segs * pairs, masked_attention)

    exchanges = []

    def twin_copy(src, dst):
        slot = len(exchanges)
        copy = remote(src, dst, x_send.at[slot], x_recv.at[slot], place.twin)
        copy.start()
        exchanges.append(copy)
        return copy

    def swap(slot, partial):
        swap_out[slot] = partial.astype(low_type)
        return twin_copy(swap_out.at[slot], swap_in.at[slot])

    def swapped(slot, copy):
        copy.wait_recv()
        return swap_out[slot].astype(full_type) + swap_in[slot].astype(full_type)

    load_o.wait()
    partial = dots(context_m[...], wo[...])
    pl.semaphore_wait(barrier, len(partners))
    swapping = swap(0, partial)

    def spread_values(i):
        s, pair = i // pairs, lax.rem(i, pairs)
        v = values[s, :, lanes(pair, 128)]
        ones = jnp.ones_like(v)
        pair_values[i, 0] = jnp.where(gate, v, ones)
        pair_values[i, 1] = jnp.where(gate, ones, v)

    repeat(segs * pairs, spread_values)

    load_i.wait()
    load_u.wait()
    scaled, inverse = norm_stats(rows_m[...].astype(full_type) + (swapped(0, swapping) + out_bias))
    first_scaled[...] = scaled
    normed = scaled * first_gain + first_shift
    normed_low = normed.astype(low_type)
    gathers = [Gather(place, all_ref, part, g_send, g_recv, t_send, t_recv) for part in range(2)]
    for part, gather in enumerate(gathers):
        all_ref[0, gather.rows(gather.own)] = normed_low[part * masked : (part + 1) * masked]
    partial = jnp.zeros((m_rows, width), full_type)
    parts = hidden // width
    for part in range(parts):
        cols = slice(part * width, (part + 1) * width)
        pre_act = dots(normed_low, wi[:, cols]) + inner_bias(part)
        share = 0.5 * (1.0 + lax.erf(pre_act * root_half))
        slope[:, cols] = share + pre_act * jnp.exp(-0.5 * pre_act * pre_act) * gauss_norm
        partial += dots((pre_act * share).astype(low_type), wu[cols])
    swapping = swap(1, partial)
    scaled2, inverse2 = norm_stats(normed + (swapped(1, swapping) + outer_bias))
    upstream = cot_ref[...].reshape(m_rows, width).astype(full_type)
    second_in_grad = norm_backward(upstream, scaled2, inverse2, second_gain)
    outer_grad = second_in_grad.astype(low_type)
    for part, gather in enumerate(gathers):
        all_ref[1, gather.rows(gather.own)] = outer_grad[part * masked : (part + 1) * masked]
    for gather in gathers:
        gather.start()
    small = SmallGather(place, small_all, s_send, s_recv)
    mine = small.line + place.z

    def column_sum(value):
        return jnp.sum(value, axis=0, keepdims=True)

    second_gain_part, second_shift_part = column_sum(upstream * scaled2), column_sum(upstream)

    partial = jnp.zeros((m_rows, width), full_type)
    for part in range(parts):
        cols = slice(part * width, (part + 1) * width)
        inner_grad = (dots(outer_grad, wu[cols], 1, 1) * slope[:, cols]).astype(low_type)
        partial += dots(inner_grad, wi[:, cols], 1, 1)
    swapping = swap(2, partial)
    for gather in gathers:
        gather.z_step(1)
    normed_grad = second_in_grad + swapped(2, swapping)
    scaled = first_scaled[...]
    first_in_grad = norm_backward(normed_grad, scaled, inverse, first_gain)
    fig[...] = first_in_grad
    attention_grad = first_in_grad.astype(low_type)
    small_all[mine, 0:1] = column_sum(attention_grad.astype(full_type))
    small_all[mine, 1:2] = column_sum(normed_grad * scaled)
    small_all[mine, 2:3] = column_sum(normed_grad)
    small_all[mine, 3:4] = second_gain_part
    small_all[mine, 4:5] = second_shift_part
    out_grad = dots(context_m[...], attention_grad, 0, 0).astype(low_type)
    grads[0, 0:half] = out_grad[:, :half]
    grads[0, half : 2 * half] = out_grad[:, half:]
    reduces = [
        Reduce(
            place, slot, grads.at[slot], sum_ref.at[slot], first.at[slot], second.at[slot], third.at[slot],
            acc.at[slot], r_send, r_recv,
        )
        for slot in range(4)
    ]
    stage[...] = dots(attention_grad, wo[...], 1, 1).astype(low_type)

    def masked_back(i):
        s, pair = i // pairs, lax.rem(i, pairs)
        m, cols = at_rows(s * masked, masked), lanes(pair, 128)
        value_cols = pl.ds(pl.multiple_of(half + pair * 128, 128), 128)
        context_grad = apart(stage[m, cols])
        share = probs[i]
        weighed = share * dots(context_grad, values[s, :, cols], 1, 1)
        score_grad = (weighed - share * jnp.sum(weighed, axis=1, keepdims=True)).astype(low_type)
        all_rows = at_rows(s * tall, tall)
        found = dots(share.astype(low_type), context_grad, 0, 0)
        kv_grad[all_rows, value_cols] = found[:tall].astype(low_type)
        found = dots(score_grad, apart(query_m[m, cols]), 0, 0) * score_scale
        kv_grad[all_rows, cols] = found[:tall].astype(low_type)
        found = dots(score_grad, keys[s, :, cols]) * score_scale
        query_grad[m, cols] = jnp.where(gate, found[:masked], found[masked:]).astype(low_type)

    repeat(segs * pairs, masked_back)
    for gather in gathers:
        gather.z_step(3)
    grads[1] = dots(rows_m[...], query_grad[...], 0, 0).astype(low_type)
    small_all[mine, 5:6] = jnp.concatenate(
        [
            column_sum(query_grad[...].astype(full_type)),
            column_sum(kv_grad[:, half:].astype(full_type)),
        ],
        axis=1,
    )
    small_all[mine, 6:8] = jnp.zeros((2, width), full_type)
    reduces[0].step_1()
    reduces[1].step_1()

    def key_value_grad(c):
        cols = lanes(c, 256)
        found = dots(rows[:, cols], kv_grad[...], 0, 0).astype(low_type)
        grads[2, cols] = found[:, :half]
        grads[3, cols] = found[:, half:]

    repeat(width // 256, key_value_grad)
    for gather in gathers:
        gather.z_step(2)
    reduces[2].step_1()
    reduces[3].step_1()
    small.step_1()

    masked_part = dots(query_grad[...], wq[...], 1, 1) + jnp.where(head == 0, fig[...], 0.0)
    high = masked_part.astype(low_type)
    rest = (masked_part - high.astype(full_type)).astype(low_type)
    for s in range(segs):
        spread[s, 0:masked] = high[s * masked : (s + 1) * masked]
        spread[s, masked : 2 * masked] = rest[s * masked : (s + 1) * masked]

    def row_grad(i):
        s, c = i // 2, lax.rem(i, 2)
        here = at_rows(s * tall + c * own_seq, own_seq)
        found = dots(kv_grad[here], wkv[...], 1, 1)
        found += dots(pick[s, :, lanes(c, own_seq)], spread[s], 0, 0)
        part_t[here] = found.astype(low_type)

    repeat(2 * segs, row_grad)
    for s in range(segs):
        here = pl.ds(s * tall + seq, mem_pad)
        part_t[here] = dots(kv_grad[here], wkv[...], 1, 1).astype(low_type)

    def send_rows(source, target, s):
        away = at_rows(s * tall + (1 - head) * own_seq, own_seq)
        one = twin_copy(source.at[away], target.at[pl.ds(s * own, own_seq)])
        two = twin_copy(source.at[pl.ds(s * tall + seq, mem_pad)], target.at[pl.ds(s * own + own_seq, mem_pad)])
        return one, two

    moved_t = [send_rows(part_t, got_t, s) for s in range(segs)]
    for gather in gathers:
        gather.p_step(0)

    pool_at = 0

    def region(count):
        nonlocal pool_at
        pool_at += count
        return pool.at[pl.ds(pool_at - count, count)]

    part_a, got_a, low_d = region(segs * tall), region(segs * own), region(segs * tall)
    part_f, got_f = region(segs * tall), region(segs * own)
    active = region(parts * tall)

    def dense_query(s):
        here = at_rows(s * tall, tall)
        query_d[here] = (dots(rows[here], wq[...]) + query_bias).astype(low_type)

    repeat(segs, dense_query)
    exp_scale = score_scale * math.log2(math.e)

    def dense_attention(s, pair):
        cols = lanes(pair, 128)
        block_rows = tall // 2
        k = keys[s, :, cols]
        for block in range(2):
            here = at_rows(s * tall + block * block_rows, block_rows)
            query = query_d[here, cols]
            zero = jnp.zeros_like(query)
            found = []
            for side in range(2):
                lone = jnp.where(gate, query, zero) if side == 0 else jnp.where(gate, zero, query)
                scores = dots(lone, k, 1, 1)
                scores = jnp.concatenate([scores[:, :seq], scores[:, seq:] + key_mask], axis=1)
                raised = jnp.exp2((scores - jnp.max(scores, axis=1, keepdims=True)) * exp_scale)
                found.append(dots(raised.astype(low_type), pair_values[s * pairs + pair, side]))
            top = jnp.where(gate, found[0], found[1])
            total = pltpu.roll(jnp.where(gate, found[1], found[0]), HDIM, 1)
            context_d[here, cols] = (top / total).astype(low_type)

    def dense_out(s):
        here = pl.ds(s * tall, tall)
        part_a[here] = dots(context_d[here], wo[...]).astype(low_type)

    def norm_first(s, local, count):
        tokens_here = at_rows(s * tall + head * own_seq + local, count)
        here = pl.ds(s * tall + seq, count) if local == own_seq else tokens_here
        near = pl.ds(s * own + local, count)
        total = part_a[here].astype(full_type) + got_a[near].astype(full_type) + out_bias
        scaled, _ = norm_stats(rows[here].astype(full_type) + total)
        value = scaled * first_gain + first_shift
        normed_d[near] = value
        low_d[here] = value.astype(low_type)

    def norm_second(s, local, count):
        tokens_here = at_rows(s * tall + head * own_seq + local, count)
        here = pl.ds(s * tall + seq, count) if local == own_seq else tokens_here
        near = pl.ds(s * own + local, count)
        total = part_f[here].astype(full_type) + got_f[near].astype(full_type) + outer_bias
        scaled, _ = norm_stats(normed_d[near] + total)
        value = (scaled * second_gain + second_shift).astype(low_type)
        if local == own_seq:
            memory_out_ref[s] = value
        else:
            layer_out_ref[s, pl.ds(local, count)] = value

    chunk = 128
    spans = [(c * chunk, chunk) for c in range(own_seq // chunk)] + [(own_seq, mem_pad)]
    gather_ticks = [("p", step) for step in Z_ORDER[1:]] + [(side, step) for side in range(2) for step in Z_ORDER]

    def tick(count=1):
        for _ in range(count):
            if not gather_ticks:
                return
            kind, step = gather_ticks.pop(0)
            for gather in gathers:
                if kind == "p":
                    gather.p_step(step)
                else:
                    gather.q_step(kind, step)

    reduce_ticks = [
        (name, pair) for name in ("step_2", "step_3", "step_4", "step_5", "step_6") for pair in (0, 2)
    ]

    def reduce_tick(count=1):
        for _ in range(count):
            if not reduce_ticks:
                return
            name, pair = reduce_ticks.pop(0)
            for reduce in reduces[pair : pair + 2]:
                getattr(reduce, name)()

    moved_a = []
    for s in range(segs):
        for pair in range(pairs):
            dense_attention(s, pair)
            tick()
        dense_out(s)
        moved_a.append(send_rows(part_a, got_a, s))
    small.step_2()
    moved_n = []
    for s in range(segs):
        for copy in moved_a[s]:
            copy.wait_recv()
        for local, count in spans:
            norm_first(s, local, count)
        ours = low_d.at[at_rows(s * tall + head * own_seq, own_seq)]
        moved_n.append(twin_copy(ours, ours))
    for s in range(segs):
        for copy in moved_t[s]:
            copy.wait_recv()
        ours = at_rows(s * tall + head * own_seq, own_seq)
        near = got_t[pl.ds(s * own, own_seq)].astype(full_type)
        tokens_grad_ref[s] = (part_t[ours].astype(full_type) + near).astype(low_type)
        near = got_t[pl.ds(s * own + own_seq, mem_pad)].astype(full_type)
        memory_grad_ref[s] = (part_t[pl.ds(s * tall + seq, mem_pad)].astype(full_type) + near).astype(low_type)
    small.step_3()
    tick()
    moved_f = []
    for s in range(segs):
        moved_n[s].wait_recv()
        here = pl.ds(s * tall, tall)
        for part in range(parts):
            cols = slice(part * width, (part + 1) * width)
            pre_act = dots(low_d[here], wi[:, cols]) + inner_bias(part)
            active[pl.ds(part * tall, tall)] = (0.5 * pre_act * (1.0 + lax.erf(pre_act * root_half))).astype(low_type)
            tick()
        partial = dots(active[pl.ds(0, tall)], wu[0:width])
        for part in range(1, parts):
            partial += dots(active[pl.ds(part * tall, tall)], wu[part * width : (part + 1) * width])
        part_f[here] = partial.astype(low_type)
        moved_f.append(send_rows(part_f, got_f, s))
        reduce_tick()
    tick(len(gather_ticks))
    for s in range(segs):
        for copy in moved_f[s]:
            copy.wait_recv()
        for local, count in spans:
            norm_second(s, local, count)
    for copy in exchanges:
        copy.wait_send()

    total_rows = all_ref.shape[1]
    active_all, inner_grad_all = pool.at[pl.ds(0, total_rows)], pool.at[pl.ds(total_rows, total_rows)]
    for gather in gathers:
        gather.all_landed()
    ones = jnp.ones((16, total_rows), low_type)
    block_rows = 512
    for part in range(parts):
        cols = slice(part * width, (part + 1) * width)

        def hidden_block(i):
            here = at_rows(i * block_rows, block_rows)
            pre_act = dots(all_ref[0, here], wi[:, cols]) + inner_bias(part)
            back = dots(all_ref[1, here], wu[cols], 1, 1)
            share = 0.5 * (1.0 + lax.erf(pre_act * root_half))
            active_all[here] = (pre_act * share).astype(low_type)
            bell = pre_act * jnp.exp(-0.5 * pre_act * pre_act) * gauss_norm
            inner_grad_all[here] = (back * (share + bell)).astype(low_type)

        repeat(total_rows // block_rows, hidden_block)
        reduce_tick(2)
        outer_grad_ref[cols] = dots(active_all[...], all_ref[1], 0, 0).astype(low_type)
        reduce_tick()
        inner_grad_ref[:, cols] = dots(all_ref[0], inner_grad_all[...], 0, 0).astype(low_type)
        vec_out_ref[8 + part : 9 + part] = dots(ones, inner_grad_all[...])[0:1]
        reduce_tick()
    vec_out_ref[10:11] = dots(ones, all_ref[1])[0:1]
    reduce_tick(len(reduce_ticks))
    small.finish()
    total = small_all[0]
    for block in range(1, GROUP):
        total += small_all[block]
    vec_out_ref[0:8] = total
    vec_out_ref[11:16] = jnp.zeros((5, width), full_type)
    for reduce in reduces:
        reduce.finish()
    for gather in gathers:
        gather.finish()


def layer(tokens, memory, weights, index, cotangent, vectors):
    segs, seq, width = tokens.shape
    mem_pad, masked = memory.shape[1], cotangent.shape[1]
    half, hidden = weights[0].shape[1], weights[4].shape[1]
    tall, own, m_rows = seq + mem_pad, seq // 2 + mem_pad, segs * masked
    key_rows = -(-tall // 128) * 128
    pairs, parts = half // 128, hidden // width
    total_rows = GROUP * m_rows
    pool_rows = max(2 * total_rows, (3 * segs + parts) * tall + 2 * segs * own)
    vmem, anywhere = pl.BlockSpec(memory_space=pltpu.VMEM), pl.BlockSpec(memory_space=pl.ANY)

    def low(*shape):
        return pltpu.VMEM(shape, low_type)

    def full(*shape):
        return pltpu.VMEM(shape, full_type)

    def result(*shape):
        return jax.ShapeDtypeStruct(shape, low_type)

    sems = pltpu.SemaphoreType.DMA
    return pl.pallas_call(
        layer_kernel,
        out_shape=(
            result(segs, seq // 2, width),
            result(segs, mem_pad, width),
            result(segs, seq // 2, width),
            result(segs, mem_pad, width),
            result(4, width, half),
            result(hidden, width),
            result(width, hidden),
            jax.ShapeDtypeStruct((16, width), full_type),
        ),
        in_specs=[anywhere] * 8 + [vmem] * 3,
        out_specs=(vmem,) * 8,
        scratch_shapes=[
            low(segs * tall, width), low(width, half), low(width, 2 * half), low(half, width),
            low(width, hidden), low(hidden, width), sems((2 * segs + 6,)),
            low(segs, 2 * masked, seq), low(segs, key_rows, half), low(segs, key_rows, half),
            low(segs * pairs, 2, key_rows, 128), low(m_rows, width), low(m_rows, half),
            full(segs * pairs, 2 * masked, key_rows), low(m_rows, half), low(3, m_rows, width), low(3, m_rows, width),
            full(m_rows, width), full(m_rows, width), full(m_rows, hidden), low(m_rows, half),
            low(segs * tall, 2 * half), low(segs, 2 * masked, width), low(m_rows, half),
            low(2, total_rows, width), full(GROUP, 8, width), low(4, width, half),
            low(4, width // 2, half), low(4, width // 4, half), low(4, 3, width // 16, half), low(4, width // 2, half),
            low(segs * tall, width), low(segs * own, width), low(segs * tall, half), low(segs * tall, half),
            full(segs * own, width), low(pool_rows, width),
            sems((2, 16)), sems((2, 16)), sems((2, 16)), sems((2, 16)), sems((4, 10)), sems((4, 10)),
            sems((5,)), sems((5,)), sems((3 + 7 * segs,)), sems((3 + 7 * segs,)),
        ],
        compiler_params=pltpu.CompilerParams(
            collective_id=0, has_side_effects=True, vmem_limit_bytes=63 * 2**20
        ),
    )(tokens, memory, *weights, index, cotangent, vectors)


def across_groups(values):
    size = lax.axis_size("dp")
    if size == GROUP:
        return values
    total = values
    moved = values
    for _ in range(size // GROUP - 1):
        moved = lax.ppermute(moved, "dp", [(i, (i + GROUP) % size) for i in range(size)])
        total = total + moved
    return total


def on_device(
    tokens,
    memory,
    query_weight,
    query_bias,
    key_weight,
    value_weight,
    value_bias,
    out_weight,
    out_bias,
    first_gain,
    first_shift,
    inner_weight,
    inner_bias,
    outer_weight,
    outer_bias,
    second_gain,
    second_shift,
    masked_rows,
    cotangent,
):
    seq_len, width = tokens.shape[1:]
    mem_len = memory.shape[1]
    mem_pad = -(-mem_len // 32) * 32
    head = lax.axis_index("head")
    half = out_weight.shape[0]
    true_keys = jnp.arange(width) < mem_len
    vectors = jnp.concatenate(
        [
            out_bias, first_gain, first_shift, outer_bias, second_gain, second_shift,
            query_bias, value_bias, jnp.zeros_like(out_bias), inner_bias,
        ]
    ).astype(full_type)
    vectors = jnp.concatenate([vectors, jnp.where(true_keys, 0.0, -1e30)]).reshape(-1, width)
    vectors = jnp.pad(vectors, ((0, 16 - vectors.shape[0]), (0, 0)))
    weights = (query_weight, key_weight, value_weight, out_weight, inner_weight, outer_weight)
    layer_out, memory_out, tokens_grad, memory_grad, sums, outer_weight_grad, inner_weight_grad, vecs = layer(
        tokens,
        jnp.pad(memory, ((0, 0), (0, mem_pad - mem_len), (0, 0))),
        weights,
        masked_rows[:, :, None],
        cotangent,
        vectors,
    )
    own_mem = mem_len // 2

    def own_memory(values):
        return lax.dynamic_slice_in_dim(values, head * own_mem, own_mem, 1)

    def grown(values):
        return across_groups(values.astype(full_type))

    sums, vecs = grown(sums), grown(vecs)
    return (
        layer_out,
        own_memory(memory_out),
        tokens_grad,
        own_memory(memory_grad),
        sums[1],
        vecs[5, :half],
        sums[2],
        sums[3],
        vecs[5, half:],
        jnp.concatenate([sums[0, :half], sums[0, half:]], axis=1),
        vecs[0],
        vecs[1],
        vecs[2],
        grown(inner_weight_grad),
        vecs[8:10].reshape(-1),
        grown(outer_weight_grad),
        vecs[10],
        vecs[3],
        vecs[4],
    )


def solution(mesh):
    return jax.shard_map(
        on_device,
        mesh=mesh,
        in_specs=(
            P("dp", None, None),
            P("dp", None, None),
            P(None, "head"),
            P("head"),
            P(None, "head"),
            P(None, "head"),
            P("head"),
            P("head", None),
            P(),
            P(),
            P(),
            P(None, "head"),
            P("head"),
            P("head", None),
            P(),
            P(),
            P(),
            P("dp", None),
            P("dp", None, None),
        ),
        out_specs=(
            P("dp", "head", None),
            P("dp", "head", None),
            P("dp", "head", None),
            P("dp", "head", None),
            P(None, "head"),
            P("head"),
            P(None, "head"),
            P(None, "head"),
            P("head"),
            P("head", None),
            P(),
            P(),
            P(),
            P(None, "head"),
            P("head"),
            P("head", None),
            P(),
            P(),
            P(),
        ),
        check_vma=False,
    )
```

```python
import math

import jax
import jax.numpy as jnp
from jax import lax
from jax.experimental import pallas as pl
from jax.experimental.pallas import tpu as pltpu
from jax.sharding import PartitionSpec as P

HDIM = 64
GROUP = 16
MESH = pl.DeviceIdType.MESH

norm_eps = 1e-12
root_half = 1.0 / math.sqrt(2.0)
gauss_norm = 1.0 / math.sqrt(2.0 * math.pi)
low_type = jnp.bfloat16
full_type = jnp.float32


def norm_stats(values):
    center = values - jnp.mean(values, axis=-1, keepdims=True)
    inverse = lax.rsqrt(jnp.mean(center * center, axis=-1, keepdims=True) + norm_eps)
    return center * inverse, inverse


def norm_backward(upstream, scaled, inverse, gain_vector):
    weighted = upstream * gain_vector
    plain_mean = jnp.mean(weighted, axis=-1, keepdims=True)
    cross_mean = jnp.mean(weighted * scaled, axis=-1, keepdims=True)
    return inverse * (weighted - plain_mean - scaled * cross_mean)


class Place:
    def __init__(self):
        index = lax.axis_index("dp")
        self.head = lax.axis_index("head")
        base = index // GROUP * GROUP
        inner = lax.rem(index, GROUP)
        self.x = lax.rem(inner, 2)
        self.y = lax.rem(inner // 2, 2)
        self.z = inner // 4
        self.base = base
        self.twin = (index, 1 - self.head)

    def at(self, x, y, z):
        return (self.base + z * 4 + y * 2 + x, self.head)

    def axes(self, flip):
        x_next = self.at(1 - self.x, self.y, self.z)
        y_next = self.at(self.x, 1 - self.y, self.z)
        if flip:
            return self.y, self.x, y_next, x_next
        return self.x, self.y, x_next, y_next

    def z_plus(self, step):
        return lax.rem(self.z + step, 4)

    def along_z(self, step):
        return self.at(self.x, self.y, self.z_plus(step))

    def partners(self):
        found = [self.twin, self.at(1 - self.x, self.y, self.z), self.at(self.x, 1 - self.y, self.z)]
        return found + [self.along_z(step) for step in (1, 2, 3)]


def remote(src, dst, send, recv, device):
    return pltpu.make_async_remote_copy(
        src_ref=src, dst_ref=dst, send_sem=send, recv_sem=recv, device_id=device, device_id_type=MESH
    )


ORDER = (
    "z1", "z2", "p0", "z3", "p1", "s2", "r02", "p2", "p3", "r12", "q00", "q01",
    "r22", "r32", "q02", "q03", "r03", "r13", "q10", "r23", "r33", "q11", "s3", "r04",
    "r14", "q12", "q13", "r24", "r34", "r05", "r15", "r25", "r35", "r06", "r16", "r26",
    "r36",
)


class Reduce:
    def __init__(self, place, slot, src_ref, out_ref, first, second, third, acc, send, recv):
        self.place, self.slot = place, slot
        self.src, self.out = src_ref, out_ref
        self.first, self.second, self.third, self.acc = first, second, third, acc
        self.send, self.recv = send, recv
        self.p, self.q, self.p_next, self.q_next = place.axes(slot % 2 == 1)
        rows = src_ref.shape[0]
        self.p_rows, self.q_rows, self.z_rows = rows // 2, rows // 4, rows // 16
        self.count = 0
        self.copies = []

    def put(self, src, dst, device):
        copy = remote(src, dst, self.send.at[self.slot, self.count], self.recv.at[self.slot, self.count], device)
        copy.start()
        self.count += 1
        self.copies.append(copy)

    def landed(self, count):
        for copy in self.copies[-count:]:
            copy.wait_recv()

    def step_1(self):
        away = (1 - self.p) * self.p_rows
        self.put(self.src.at[pl.ds(away, self.p_rows)], self.first, self.p_next)

    def step_2(self):
        self.landed(1)
        kept = self.src[pl.ds(self.p * self.p_rows, self.p_rows)].astype(full_type)
        self.acc[...] = (kept + self.first[...].astype(full_type)).astype(low_type)
        away = (1 - self.q) * self.q_rows
        self.put(self.acc.at[pl.ds(away, self.q_rows)], self.second, self.q_next)

    def step_3(self):
        self.landed(1)
        mine = pl.ds(self.q * self.q_rows, self.q_rows)
        kept = self.acc[mine].astype(full_type)
        self.acc[mine] = (kept + self.second[...].astype(full_type)).astype(low_type)
        for step in (1, 3, 2):
            away = self.q * self.q_rows + self.place.z_plus(step) * self.z_rows
            self.put(self.acc.at[pl.ds(away, self.z_rows)], self.third.at[step - 1], self.place.along_z(step))

    def span(self):
        return self.p * self.p_rows + self.q * self.q_rows + self.place.z * self.z_rows

    def step_4(self):
        self.landed(3)
        total = self.acc[pl.ds(self.q * self.q_rows + self.place.z * self.z_rows, self.z_rows)].astype(full_type)
        for step in range(3):
            total += self.third[step].astype(full_type)
        mine = pl.ds(self.span(), self.z_rows)
        self.out[mine] = total.astype(low_type)
        for step in (1, 3, 2):
            self.put(self.out.at[mine], self.out.at[mine], self.place.along_z(step))

    def step_5(self):
        self.landed(3)
        mine = pl.ds(self.p * self.p_rows + self.q * self.q_rows, self.q_rows)
        self.put(self.out.at[mine], self.out.at[mine], self.q_next)

    def step_6(self):
        self.landed(1)
        mine = pl.ds(self.p * self.p_rows, self.p_rows)
        self.put(self.out.at[mine], self.out.at[mine], self.p_next)

    def finish(self):
        self.landed(1)
        for copy in self.copies:
            copy.wait_send()


class SmallGather:
    def __init__(self, place, all_ref, send, recv):
        self.place, self.all, self.send, self.recv = place, all_ref, send, recv
        self.line = (place.y * 2 + place.x) * 4
        self.copies = []

    def put(self, start, count, device):
        ref = self.all.at[pl.ds(start, count)]
        slot = len(self.copies)
        copy = remote(ref, ref, self.send.at[slot], self.recv.at[slot], device)
        copy.start()
        self.copies.append(copy)

    def step_1(self):
        for step in (1, 2, 3):
            self.put(self.line + self.place.z, 1, self.place.along_z(step))

    def step_2(self):
        for step in (1, 2, 3):
            ref = self.all.at[pl.ds(self.line + self.place.z_plus(step), 1)]
            remote(ref, ref, self.send.at[0], self.recv.at[3 - step], self.place.along_z(step)).wait_recv()
        self.put(self.line, 4, self.place.at(1 - self.place.x, self.place.y, self.place.z))

    def step_3(self):
        self.copies[3].wait_recv()
        self.put(self.place.y * 8, 8, self.place.at(self.place.x, 1 - self.place.y, self.place.z))

    def finish(self):
        self.copies[4].wait_recv()
        for copy in self.copies:
            copy.wait_send()


def dots(left, right, left_dim=1, right_dim=0):
    return lax.dot_general(
        left, right, (((left_dim,), (right_dim,)), ((), ())), preferred_element_type=full_type
    )


def at_rows(start, count):
    return pl.ds(pl.multiple_of(start, 16), count)


def lanes(index, count):
    return pl.ds(pl.multiple_of(index * count, count), count)


def repeat(count, body):
    def step(index, carry):
        body(index)
        return carry

    lax.fori_loop(0, count, step, 0)


class Gather:
    def __init__(self, place, all_ref, half, send, recv, twin_recv):
        self.place, self.all, self.half = place, all_ref, half
        self.size = all_ref.shape[1] // (2 * GROUP)
        self.send, self.recv, self.twin_recv = send, recv, twin_recv
        self.p, self.q, self.p_next, self.q_next = place.axes(half == 1)
        self.own = self.block(self.q, self.p, place.z)
        self.sends = []
        z = place.z
        far = z // 2
        self.z_from = (z, 1 - z + 4 * far, 2 - far, 3 - 3 * far)
        inward, outward = 1 + lax.rem(z, 2), lax.rem(3 * z - 3 + 12, 12)
        self.inward, self.outward = place.at(place.x, place.y, inward), place.at(place.x, place.y, outward)
        across = place.at(place.x, place.y, 3 - z)
        self.z_next = (None, across, self.outward, self.outward)
        self.between = lax.rem(z, 3) != 0

    def block(self, q, p, z):
        return (q * 2 + p) * 4 + z

    def rows(self, block):
        return at_rows((self.half * GROUP + block) * self.size, self.size)

    def ref(self, block, kind):
        return self.all.at[kind, self.rows(block)]

    def pass_on(self, block, device, only=None):
        slot = len(self.sends)

        def copy():
            ref = self.ref(block, self.place.head)
            return remote(ref, ref, self.send.at[self.half, slot], self.recv.at[self.half, block], device)

        self.sends.append((copy, only))
        if only is None:
            copy().start()
        else:
            pl.when(only)(lambda: copy().start())

    def to_twin(self, block):
        slot = len(self.sends)

        def copy():
            ref = self.ref(block, self.place.head)
            return remote(ref, ref, self.send.at[self.half, slot], self.twin_recv.at[self.half, block], self.place.twin)

        self.sends.append((copy, None))
        copy().start()

    def landed(self, block):
        ref = self.ref(block, self.place.head)
        remote(ref, ref, self.send.at[self.half, 0], self.recv.at[self.half, block], self.p_next).wait_recv()

    def start(self):
        self.sends.clear()
        self.pass_on(self.own, self.inward)
        self.pass_on(self.own, self.outward, self.between)
        self.pass_on(self.own, self.p_next)
        self.pass_on(self.own, self.q_next)

    def z_step(self, step):
        block = self.block(self.q, self.p, self.z_from[step])
        self.landed(block)
        self.pass_on(block, self.z_next[step], self.between)
        self.pass_on(block, self.p_next)
        self.pass_on(block, self.q_next)
        self.to_twin(block)

    def p_step(self, step):
        block = self.block(self.q, 1 - self.p, self.z_from[step])
        self.landed(block)
        self.pass_on(block, self.q_next)
        self.to_twin(block)

    def q_step(self, side, step):
        p = self.p if side == 0 else 1 - self.p
        block = self.block(1 - self.q, p, self.z_from[step])
        self.landed(block)
        self.to_twin(block)

    def all_landed(self):
        kind = 1 - self.place.head
        for side in range(2):
            for other in range(2):
                for step in range(4):
                    if side + other + step == 0:
                        continue
                    q = self.q if side == 0 else 1 - self.q
                    p = self.p if other == 0 else 1 - self.p
                    block = self.block(q, p, self.z_from[step])
                    ref = self.ref(block, kind)
                    remote(
                        ref, ref, self.send.at[self.half, 0], self.twin_recv.at[self.half, block], self.place.twin
                    ).wait_recv()

    def finish(self):
        for copy, only in self.sends:
            if only is None:
                copy().wait_send()
            else:
                pl.when(only)(lambda copy=copy: copy().wait_send())


def layer_kernel(
    tokens_any, query_any, key_any, value_any, out_any, inner_any, outer_any,
    memory_ref, index_ref, cot_ref, query_bias_ref, value_bias_ref, out_bias_ref, first_gain_ref, first_shift_ref,
    inner_bias_ref, outer_bias_ref, second_gain_ref, second_shift_ref,
    layer_out_ref, memory_out_ref, tokens_grad_ref, memory_grad_ref, sum_ref, outer_grad_ref, inner_grad_ref,
    vec_out_ref,
    rows, wq, wkv, wo, wi, wu, load_sem,
    pick, keys, values, pair_values, rows_m, query_m, probs, context_m, swap_out, swap_in,
    first_scaled, fig, slope, query_grad, kv_grad, spread, stage,
    all_ref, small_all, grads, first, second, third, acc,
    part_t, got_t, query_d, context_d, normed_d, pool,
    g_send, g_recv, t_recv, r_send, r_recv, s_send, s_recv, x_send, x_recv,
):
    segs, seq, width = tokens_any.shape
    mem_len = memory_ref.shape[0]
    mem_pad = -(-mem_len // 32) * 32
    tall = seq + mem_pad
    masked = cot_ref.shape[1]
    m_rows = segs * masked
    own_seq = seq // 2
    own = own_seq + mem_pad
    half = query_any.shape[1]
    pairs = half // 128
    key_rows = keys.shape[1]
    hidden = inner_any.shape[1]
    place = Place()
    head = place.head
    gate = lax.broadcasted_iota(jnp.int32, (1, 128), 1) < HDIM
    score_scale = 1.0 / math.sqrt(HDIM)

    loads = []

    def load(src, dst):
        copy = pltpu.make_async_copy(src, dst, load_sem.at[len(loads)])
        copy.start()
        loads.append(copy)
        return copy

    load_rows = []
    for s in range(segs):
        load_rows.append(load(tokens_any.at[s], rows.at[pl.ds(s * tall, seq)]))
    load_kv = [load(key_any, wkv.at[:, pl.ds(0, half)]), load(value_any, wkv.at[:, pl.ds(half, half)])]
    load_q, load_o = load(query_any, wq), load(out_any, wo)
    load_i, load_u = load(inner_any, wi), load(outer_any, wu)

    barrier = pltpu.get_barrier_semaphore()
    partners = place.partners()
    for partner in partners:
        pl.semaphore_signal(barrier, inc=1, device_id=partner, device_id_type=MESH)

    def vector(ref, start=0, count=None):
        count = ref.shape[0] if count is None else count
        return ref[pl.ds(start, count)].astype(full_type).reshape(1, count)

    out_bias, first_gain, first_shift = vector(out_bias_ref), vector(first_gain_ref), vector(first_shift_ref)
    outer_bias, second_gain, second_shift = vector(outer_bias_ref), vector(second_gain_ref), vector(second_shift_ref)
    query_bias, value_bias = vector(query_bias_ref), vector(value_bias_ref)
    key_index = lax.broadcasted_iota(jnp.int32, (1, key_rows - seq), 1)
    key_mask = jnp.where(key_index < mem_len, 0.0, -1e30).astype(full_type)

    def inner_bias(part):
        return vector(inner_bias_ref, part * width, width)

    memory = memory_ref[...].astype(full_type)
    blank = jnp.zeros((mem_pad - mem_len, width), full_type)
    for s in range(segs):
        filled = jnp.concatenate([memory[:, s, :], blank], axis=0)
        rows[pl.ds(s * tall + seq, mem_pad)] = filled.astype(low_type)
    keys[:, pl.ds(tall, key_rows - tall)] = jnp.zeros((segs, key_rows - tall, half), low_type)
    values[:, pl.ds(tall, key_rows - tall)] = jnp.zeros((segs, key_rows - tall, half), low_type)
    for s in range(segs):
        hot = index_ref[s : s + 1] == lax.broadcasted_iota(jnp.int32, (seq, masked), 0)
        pick[s] = jnp.where(hot, 1.0, 0.0).astype(low_type)

    for copy in load_rows + load_kv:
        copy.wait()

    def key_value(s):
        both = dots(rows[at_rows(s * tall, tall)], wkv[...])
        keys[s, 0:tall] = both[:, :half].astype(low_type)
        values[s, 0:tall] = (both[:, half:] + value_bias).astype(low_type)

    repeat(segs, key_value)

    load_q.wait()
    for s in range(segs):
        m = pl.ds(s * masked, masked)
        found = dots(pick[s], rows[pl.ds(s * tall, seq)], 0, 0).astype(low_type)
        rows_m[m] = found
    query_m[...] = (dots(rows_m[...], wq[...]) + query_bias).astype(low_type)

    def apart(pair):
        zero = jnp.zeros_like(pair)
        return jnp.concatenate([jnp.where(gate, pair, zero), jnp.where(gate, zero, pair)], axis=0)

    def masked_attention(i):
        s, pair = i // pairs, lax.rem(i, pairs)
        m, cols = at_rows(s * masked, masked), lanes(pair, 128)
        scores = dots(apart(query_m[m, cols]), keys[s, :, cols], 1, 1) * score_scale
        scores = jnp.concatenate([scores[:, :seq], scores[:, seq:] + key_mask], axis=1)
        raised = jnp.exp(scores - jnp.max(scores, axis=1, keepdims=True))
        share = raised / jnp.sum(raised, axis=1, keepdims=True)
        probs[i] = share
        found = dots(share.astype(low_type), values[s, :, cols])
        context_m[m, cols] = jnp.where(gate, found[:masked], found[masked:]).astype(low_type)

    repeat(segs * pairs, masked_attention)

    exchanges = []

    def twin_copy(src, dst):
        slot = len(exchanges)
        copy = remote(src, dst, x_send.at[slot], x_recv.at[slot], place.twin)
        copy.start()
        exchanges.append(copy)
        return copy

    def swap(slot, partial):
        swap_out[slot] = partial.astype(low_type)
        return twin_copy(swap_out.at[slot], swap_in.at[slot])

    def swapped(slot, copy):
        copy.wait_recv()
        return swap_out[slot].astype(full_type) + swap_in[slot].astype(full_type)

    load_o.wait()
    partial = dots(context_m[...], wo[...])
    pl.semaphore_wait(barrier, len(partners))
    swapping = swap(0, partial)

    def spread_values(i):
        s, pair = i // pairs, lax.rem(i, pairs)
        v = values[s, :, lanes(pair, 128)]
        ones = jnp.ones_like(v)
        pair_values[i, 0] = jnp.where(gate, v, ones)
        pair_values[i, 1] = jnp.where(gate, ones, v)

    repeat(segs * pairs, spread_values)

    load_i.wait()
    load_u.wait()
    scaled, inverse = norm_stats(rows_m[...].astype(full_type) + (swapped(0, swapping) + out_bias))
    first_scaled[...] = scaled
    normed = scaled * first_gain + first_shift
    normed_low = normed.astype(low_type)
    gathers = [Gather(place, all_ref, part, g_send, g_recv, t_recv) for part in range(2)]
    for part, gather in enumerate(gathers):
        all_ref[0, gather.rows(gather.own)] = normed_low[part * masked : (part + 1) * masked]
    @pl.when(head == 0)
    def _():
        for gather in gathers:
            gather.start()

    partial = jnp.zeros((m_rows, width), full_type)
    parts = hidden // width
    for part in range(parts):
        cols = slice(part * width, (part + 1) * width)
        pre_act = dots(normed_low, wi[:, cols]) + inner_bias(part)
        share = 0.5 * (1.0 + lax.erf(pre_act * root_half))
        slope[:, cols] = share + pre_act * jnp.exp(-0.5 * pre_act * pre_act) * gauss_norm
        partial += dots((pre_act * share).astype(low_type), wu[cols])
    swapping = swap(1, partial)
    scaled2, inverse2 = norm_stats(normed + (swapped(1, swapping) + outer_bias))
    upstream = cot_ref[...].reshape(m_rows, width).astype(full_type)
    second_in_grad = norm_backward(upstream, scaled2, inverse2, second_gain)
    outer_grad = second_in_grad.astype(low_type)
    for part, gather in enumerate(gathers):
        all_ref[1, gather.rows(gather.own)] = outer_grad[part * masked : (part + 1) * masked]

    @pl.when(head == 1)
    def _():
        for gather in gathers:
            gather.start()

    small = SmallGather(place, small_all, s_send, s_recv)
    mine = small.line + place.z
    reduces = [
        Reduce(
            place, slot, grads.at[slot], sum_ref.at[slot], first.at[slot], second.at[slot], third.at[slot],
            acc.at[slot], r_send, r_recv,
        )
        for slot in range(4)
    ]
    events = list(ORDER)

    def tick(count=1):
        for _ in range(min(count, len(events))):
            event = events.pop(0)
            if event[0] == "r":
                getattr(reduces[int(event[1])], "step_" + event[2])()
            elif event[0] == "s":
                getattr(small, "step_" + event[1])()
            else:
                for gather in gathers:
                    if event[0] == "z":
                        gather.z_step(int(event[1]))
                    elif event[0] == "p":
                        gather.p_step(int(event[1]))
                    else:
                        gather.q_step(int(event[1]), int(event[2]))


    def column_sum(value):
        return jnp.sum(value, axis=0, keepdims=True)

    second_gain_part, second_shift_part = column_sum(upstream * scaled2), column_sum(upstream)

    partial = jnp.zeros((m_rows, width), full_type)
    for part in range(parts):
        cols = slice(part * width, (part + 1) * width)
        inner_grad = (dots(outer_grad, wu[cols], 1, 1) * slope[:, cols]).astype(low_type)
        partial += dots(inner_grad, wi[:, cols], 1, 1)
    swapping = swap(2, partial)
    tick()
    normed_grad = second_in_grad + swapped(2, swapping)
    scaled = first_scaled[...]
    first_in_grad = norm_backward(normed_grad, scaled, inverse, first_gain)
    fig[...] = first_in_grad
    attention_grad = first_in_grad.astype(low_type)
    small_all[mine, 0:1] = column_sum(attention_grad.astype(full_type))
    small_all[mine, 1:2] = column_sum(normed_grad * scaled)
    small_all[mine, 2:3] = column_sum(normed_grad)
    small_all[mine, 3:4] = second_gain_part
    small_all[mine, 4:5] = second_shift_part
    out_grad = dots(context_m[...], attention_grad, 0, 0).astype(low_type)
    grads[0, 0:half] = out_grad[:, :half]
    grads[0, half : 2 * half] = out_grad[:, half:]
    reduces[0].step_1()
    stage[...] = dots(attention_grad, wo[...], 1, 1).astype(low_type)

    def masked_back(i):
        s, pair = i // pairs, lax.rem(i, pairs)
        m, cols = at_rows(s * masked, masked), lanes(pair, 128)
        value_cols = pl.ds(pl.multiple_of(half + pair * 128, 128), 128)
        context_grad = apart(stage[m, cols])
        share = probs[i]
        weighed = share * dots(context_grad, values[s, :, cols], 1, 1)
        score_grad = (weighed - share * jnp.sum(weighed, axis=1, keepdims=True)).astype(low_type)
        all_rows = at_rows(s * tall, tall)
        found = dots(share.astype(low_type), context_grad, 0, 0)
        kv_grad[all_rows, value_cols] = found[:tall].astype(low_type)
        found = dots(score_grad, apart(query_m[m, cols]), 0, 0) * score_scale
        kv_grad[all_rows, cols] = found[:tall].astype(low_type)
        found = dots(score_grad, keys[s, :, cols]) * score_scale
        query_grad[m, cols] = jnp.where(gate, found[:masked], found[masked:]).astype(low_type)

    repeat(segs * pairs, masked_back)
    tick()
    grads[1] = dots(rows_m[...], query_grad[...], 0, 0).astype(low_type)
    small_all[mine, 5:6] = jnp.concatenate(
        [
            column_sum(query_grad[...].astype(full_type)),
            column_sum(kv_grad[:, half:].astype(full_type)),
        ],
        axis=1,
    )
    small_all[mine, 6:8] = jnp.zeros((2, width), full_type)
    reduces[1].step_1()

    def key_value_grad(c):
        cols = lanes(c, 256)
        found = dots(rows[:, cols], kv_grad[...], 0, 0).astype(low_type)
        grads[2, cols] = found[:, :half]
        grads[3, cols] = found[:, half:]

    repeat(width // 256, key_value_grad)
    tick()
    reduces[2].step_1()
    reduces[3].step_1()
    small.step_1()

    masked_part = dots(query_grad[...], wq[...], 1, 1) + jnp.where(head == 0, fig[...], 0.0)
    high = masked_part.astype(low_type)
    rest = (masked_part - high.astype(full_type)).astype(low_type)
    for s in range(segs):
        spread[s, 0:masked] = high[s * masked : (s + 1) * masked]
        spread[s, masked : 2 * masked] = rest[s * masked : (s + 1) * masked]

    def row_grad(i):
        s, c = i // 2, lax.rem(i, 2)
        here = at_rows(s * tall + c * own_seq, own_seq)
        found = dots(kv_grad[here], wkv[...], 1, 1)
        chosen = pick[s, at_rows(c * own_seq, own_seq)]
        found += dots(chosen, spread[s, 0:masked]) + dots(chosen, spread[s, masked : 2 * masked])
        part_t[here] = found.astype(low_type)

    repeat(segs, row_grad)
    tick()
    repeat(segs, lambda i: row_grad(i + segs))
    for s in range(segs):
        here = pl.ds(s * tall + seq, mem_pad)
        part_t[here] = dots(kv_grad[here], wkv[...], 1, 1).astype(low_type)

    def send_rows(source, target, s):
        away = at_rows(s * tall + (1 - head) * own_seq, own_seq)
        one = twin_copy(source.at[away], target.at[pl.ds(s * own, own_seq)])
        two = twin_copy(source.at[pl.ds(s * tall + seq, mem_pad)], target.at[pl.ds(s * own + own_seq, mem_pad)])
        return one, two

    moved_t = [send_rows(part_t, got_t, s) for s in range(segs)]
    tick()

    pool_at = 0

    def region(count):
        nonlocal pool_at
        pool_at += count
        return pool.at[pl.ds(pool_at - count, count)]

    part_a, got_a, low_d = region(segs * tall), region(segs * own), region(segs * tall)
    part_f, got_f = region(segs * tall), region(segs * own)
    active = region(parts * tall)

    def dense_query(s):
        here = at_rows(s * tall, tall)
        query_d[here] = (dots(rows[here], wq[...]) + query_bias).astype(low_type)

    repeat(segs, dense_query)
    exp_scale = score_scale * math.log2(math.e)

    def dense_attention(s, pair):
        cols = lanes(pair, 128)
        block_rows = tall // 2
        k = keys[s, :, cols]
        for block in range(2):
            here = at_rows(s * tall + block * block_rows, block_rows)
            query = query_d[here, cols]
            zero = jnp.zeros_like(query)
            found = []
            for side in range(2):
                lone = jnp.where(gate, query, zero) if side == 0 else jnp.where(gate, zero, query)
                scores = dots(lone, k, 1, 1)
                scores = jnp.concatenate([scores[:, :seq], scores[:, seq:] + key_mask], axis=1)
                raised = jnp.exp2((scores - jnp.max(scores, axis=1, keepdims=True)) * exp_scale)
                found.append(dots(raised.astype(low_type), pair_values[s * pairs + pair, side]))
            top = jnp.where(gate, found[0], found[1])
            total = pltpu.roll(jnp.where(gate, found[1], found[0]), HDIM, 1)
            context_d[here, cols] = (top / total).astype(low_type)

    def dense_out(s):
        here = pl.ds(s * tall, tall)
        part_a[here] = dots(context_d[here], wo[...]).astype(low_type)

    def norm_first(s, local, count):
        tokens_here = at_rows(s * tall + head * own_seq + local, count)
        here = pl.ds(s * tall + seq, count) if local == own_seq else tokens_here
        near = pl.ds(s * own + local, count)
        total = part_a[here].astype(full_type) + got_a[near].astype(full_type) + out_bias
        scaled, _ = norm_stats(rows[here].astype(full_type) + total)
        value = scaled * first_gain + first_shift
        normed_d[near] = value
        low_d[here] = value.astype(low_type)

    def norm_second(s, local, count):
        tokens_here = at_rows(s * tall + head * own_seq + local, count)
        here = pl.ds(s * tall + seq, count) if local == own_seq else tokens_here
        near = pl.ds(s * own + local, count)
        total = part_f[here].astype(full_type) + got_f[near].astype(full_type) + outer_bias
        scaled, _ = norm_stats(normed_d[near] + total)
        value = (scaled * second_gain + second_shift).astype(low_type)
        if local == own_seq:
            memory_out_ref[s] = value
        else:
            layer_out_ref[s, pl.ds(local, count)] = value

    chunk = 128
    spans = [(c * chunk, chunk) for c in range(own_seq // chunk)] + [(own_seq, mem_pad)]
    moved_a = []
    for s in range(segs):
        for pair in range(pairs):
            dense_attention(s, pair)
            tick()
        dense_out(s)
        moved_a.append(send_rows(part_a, got_a, s))
    moved_n = []
    for s in range(segs):
        for copy in moved_a[s]:
            copy.wait_recv()
        for local, count in spans:
            norm_first(s, local, count)
        ours = low_d.at[at_rows(s * tall + head * own_seq, own_seq)]
        moved_n.append(twin_copy(ours, ours))
    for s in range(segs):
        for copy in moved_t[s]:
            copy.wait_recv()
        ours = at_rows(s * tall + head * own_seq, own_seq)
        near = got_t[pl.ds(s * own, own_seq)].astype(full_type)
        tokens_grad_ref[s] = (part_t[ours].astype(full_type) + near).astype(low_type)
        near = got_t[pl.ds(s * own + own_seq, mem_pad)].astype(full_type)
        memory_grad_ref[s] = (part_t[pl.ds(s * tall + seq, mem_pad)].astype(full_type) + near).astype(low_type)
    tick()
    moved_f = []
    for s in range(segs):
        moved_n[s].wait_recv()
        here = pl.ds(s * tall, tall)
        for part in range(parts):
            cols = slice(part * width, (part + 1) * width)
            pre_act = dots(low_d[here], wi[:, cols]) + inner_bias(part)
            active[pl.ds(part * tall, tall)] = (0.5 * pre_act * (1.0 + lax.erf(pre_act * root_half))).astype(low_type)
            tick()
        partial = dots(active[pl.ds(0, tall)], wu[0:width])
        for part in range(1, parts):
            partial += dots(active[pl.ds(part * tall, tall)], wu[part * width : (part + 1) * width])
        part_f[here] = partial.astype(low_type)
        moved_f.append(send_rows(part_f, got_f, s))
        tick()
    for s in range(segs):
        for copy in moved_f[s]:
            copy.wait_recv()
        for local, count in spans:
            norm_second(s, local, count)
        tick()
    for copy in exchanges:
        copy.wait_send()
    while any(event[0] in "zpq" for event in events):
        tick()

    total_rows = all_ref.shape[1]
    active_all, inner_grad_all = pool.at[pl.ds(0, total_rows)], pool.at[pl.ds(total_rows, total_rows)]
    for gather in gathers:
        gather.all_landed()
    ones = jnp.ones((16, total_rows), low_type)
    block_rows = total_rows // 4
    for part in range(parts):
        cols = slice(part * width, (part + 1) * width)

        def hidden_block(i):
            here = at_rows(i * block_rows, block_rows)
            pre_act = dots(all_ref[0, here], wi[:, cols]) + inner_bias(part)
            back = dots(all_ref[1, here], wu[cols], 1, 1)
            share = 0.5 * (1.0 + lax.erf(pre_act * root_half))
            active_all[here] = (pre_act * share).astype(low_type)
            bell = pre_act * jnp.exp(-0.5 * pre_act * pre_act) * gauss_norm
            inner_grad_all[here] = (back * (share + bell)).astype(low_type)

        def second_half(i):
            hidden_block(i + total_rows // block_rows // 2)

        repeat(total_rows // block_rows // 2, hidden_block)
        tick(3)
        repeat(total_rows // block_rows // 2, second_half)
        tick(3)
        outer_grad_ref[cols] = dots(active_all[...], all_ref[1], 0, 0).astype(low_type)
        tick(3)
        inner_grad_ref[:, cols] = dots(all_ref[0], inner_grad_all[...], 0, 0).astype(low_type)
        vec_out_ref[8 + part : 9 + part] = dots(ones, inner_grad_all[...])[0:1]
        tick(3)
    vec_out_ref[10:11] = dots(ones, all_ref[1])[0:1]
    tick(len(events))
    small.finish()
    total = small_all[0]
    for block in range(1, GROUP):
        total += small_all[block]
    vec_out_ref[0:8] = total
    vec_out_ref[11:16] = jnp.zeros((5, width), full_type)
    for reduce in reduces:
        reduce.finish()
    for gather in gathers:
        gather.finish()


def layer(tokens, memory, weights, index, cotangent, vectors):
    segs, seq, width = tokens.shape
    mem_pad, masked = -(-memory.shape[0] // 32) * 32, cotangent.shape[1]
    half, hidden = weights[0].shape[1], weights[4].shape[1]
    tall, own, m_rows = seq + mem_pad, seq // 2 + mem_pad, segs * masked
    key_rows = -(-tall // 128) * 128
    pairs, parts = half // 128, hidden // width
    total_rows = GROUP * m_rows
    pool_rows = max(2 * total_rows, (3 * segs + parts) * tall + 2 * segs * own)
    vmem, anywhere = pl.BlockSpec(memory_space=pltpu.VMEM), pl.BlockSpec(memory_space=pl.ANY)

    def low(*shape):
        return pltpu.VMEM(shape, low_type)

    def full(*shape):
        return pltpu.VMEM(shape, full_type)

    def result(*shape):
        return jax.ShapeDtypeStruct(shape, low_type)

    sems = pltpu.SemaphoreType.DMA
    return pl.pallas_call(
        layer_kernel,
        out_shape=(
            result(segs, seq // 2, width),
            result(segs, mem_pad, width),
            result(segs, seq // 2, width),
            result(segs, mem_pad, width),
            result(4, width, half),
            result(hidden, width),
            result(width, hidden),
            jax.ShapeDtypeStruct((16, width), full_type),
        ),
        in_specs=[anywhere] * 7 + [vmem] * (3 + len(vectors)),
        out_specs=(vmem,) * 8,
        scratch_shapes=[
            low(segs * tall, width), low(width, half), low(width, 2 * half), low(half, width),
            low(width, hidden), low(hidden, width), sems((segs + 6,)),
            low(segs, seq, masked), low(segs, key_rows, half), low(segs, key_rows, half),
            low(segs * pairs, 2, key_rows, 128), low(m_rows, width), low(m_rows, half),
            full(segs * pairs, 2 * masked, key_rows), low(m_rows, half), low(3, m_rows, width), low(3, m_rows, width),
            full(m_rows, width), full(m_rows, width), full(m_rows, hidden), low(m_rows, half),
            low(segs * tall, 2 * half), low(segs, 2 * masked, width), low(m_rows, half),
            low(2, total_rows, width), full(GROUP, 8, width), low(4, width, half),
            low(4, width // 2, half), low(4, width // 4, half), low(4, 3, width // 16, half), low(4, width // 2, half),
            low(segs * tall, width), low(segs * own, width), low(segs * tall, half), low(segs * tall, half),
            full(segs * own, width), low(pool_rows, width),
            sems((2, 40)), sems((2, 16)), sems((2, 16)), sems((4, 10)), sems((4, 10)),
            sems((5,)), sems((5,)), sems((3 + 7 * segs,)), sems((3 + 7 * segs,)),
        ],
        compiler_params=pltpu.CompilerParams(
            collective_id=0, has_side_effects=True, vmem_limit_bytes=63 * 2**20
        ),
    )(tokens, *weights, memory, index, cotangent, *vectors)


def result_kernel(
    layer_in, memory_in, tokens_in, memory_grad_in, out_a, out_b, query_in, key_in, value_in, outer_in, inner_in, vecs,
    layer_out, memory_out, tokens_grad, memory_grad, query_grad, query_bias, key_grad, value_grad, value_bias,
    out_grad, out_bias, first_gain, first_shift, inner_grad, inner_bias, outer_grad, outer_bias, second_gain, second_shift,
):
    layer_out[...] = layer_in[...]
    tokens_grad[...] = tokens_in[...]
    half = query_grad.shape[1]
    out_grad[:, :half] = out_a[0].astype(full_type)
    out_grad[:, half:] = out_b[0].astype(full_type)
    query_grad[...] = query_in[0].astype(full_type)
    key_grad[...] = key_in[0].astype(full_type)
    value_grad[...] = value_in[0].astype(full_type)
    inner_grad[...] = inner_in[...].astype(full_type)
    outer_grad[...] = outer_in[...].astype(full_type)

    @pl.when(pl.program_id(0) == 0)
    def _():
        count = memory_out.shape[0]
        upper = lax.axis_index("head") > 0
        for source, target in ((memory_in, memory_out), (memory_grad_in, memory_grad)):
            for s in range(source.shape[0]):
                value = source[s].astype(full_type)
                target[:, s] = jnp.where(upper, value[count : 2 * count], value[:count]).astype(low_type)
        for row, target in enumerate((out_bias, first_gain, first_shift, second_gain, second_shift)):
            target[...] = vecs[row]
        query_bias[...] = vecs[5, :half]
        value_bias[...] = vecs[5, half:]
        width = vecs.shape[1]
        for part in range(inner_bias.shape[0] // width):
            inner_bias[pl.ds(part * width, width)] = vecs[8 + part]
        outer_bias[...] = vecs[10]


def results(layer_out, memory_out, tokens_grad, memory_grad, sums, outer_grad, inner_grad, vecs, own_mem):
    segs, own_seq, width = layer_out.shape
    hidden, half = outer_grad.shape[0], sums.shape[2]
    steps = 8

    def rows_of(shape, dim):
        block = tuple(size // steps if i == dim else size for i, size in enumerate(shape))
        return pl.BlockSpec(block, lambda i: tuple(i if d == dim else 0 for d in range(len(shape))))

    def whole(*shape):
        return pl.BlockSpec(shape, lambda i: (0,) * len(shape))

    def part_of_sums(slot, rows, offset=0):
        return pl.BlockSpec((1, rows, half), lambda i: (slot, i + offset, 0))

    def full(*shape):
        return jax.ShapeDtypeStruct(shape, full_type)

    out_rows = half // steps
    moved = rows_of(layer_out.shape, 1)
    memory_shape = (own_mem, segs, width)
    square, tall, wide, out = (width, half), (hidden, width), (width, hidden), (half, width)
    shapes = (
        jax.ShapeDtypeStruct(layer_out.shape, low_type),
        jax.ShapeDtypeStruct(memory_shape, low_type),
        jax.ShapeDtypeStruct(layer_out.shape, low_type),
        jax.ShapeDtypeStruct(memory_shape, low_type),
        full(*square), full(half), full(*square), full(*square), full(half), full(*out), full(width), full(width),
        full(width), full(*wide), full(hidden), full(*tall), full(width), full(width), full(width),
    )
    specs = tuple(
        moved if i in (0, 2) else rows_of(shape.shape, 0) if len(shape.shape) == 2 else whole(*shape.shape)
        for i, shape in enumerate(shapes)
    )
    return pl.pallas_call(
        result_kernel,
        grid=(steps,),
        out_shape=shapes,
        in_specs=[
            moved, whole(*memory_out.shape), moved, whole(*memory_out.shape),
            part_of_sums(0, out_rows), part_of_sums(0, out_rows, steps),
            part_of_sums(1, width // steps), part_of_sums(2, width // steps), part_of_sums(3, width // steps),
            rows_of(tall, 0), rows_of(wide, 0), whole(*vecs.shape),
        ],
        out_specs=specs,
        compiler_params=pltpu.CompilerParams(vmem_limit_bytes=63 * 2**20),
    )(
        layer_out, memory_out, tokens_grad, memory_grad, sums, sums, sums, sums, sums, outer_grad, inner_grad, vecs
    )


def across_groups(values):
    size = lax.axis_size("dp")
    if size == GROUP:
        return values
    total = moved = values.astype(full_type)
    for _ in range(size // GROUP - 1):
        moved = lax.ppermute(moved, "dp", [(i, (i + GROUP) % size) for i in range(size)])
        total = total + moved
    return total


def on_device(
    tokens,
    memory,
    query_weight,
    query_bias,
    key_weight,
    value_weight,
    value_bias,
    out_weight,
    out_bias,
    first_gain,
    first_shift,
    inner_weight,
    inner_bias,
    outer_weight,
    outer_bias,
    second_gain,
    second_shift,
    masked_rows,
    cotangent,
):
    vectors = (
        query_bias, value_bias, out_bias, first_gain, first_shift, inner_bias, outer_bias, second_gain, second_shift,
    )
    weights = (query_weight, key_weight, value_weight, out_weight, inner_weight, outer_weight)
    rows = layer(tokens, jnp.swapaxes(memory, 0, 1), weights, masked_rows, cotangent, vectors)
    sums = tuple(across_groups(values) for values in rows[4:])
    outputs = list(results(*rows[:4], *sums, memory.shape[1] // 2))
    outputs[1], outputs[3] = jnp.swapaxes(outputs[1], 0, 1), jnp.swapaxes(outputs[3], 0, 1)
    return tuple(outputs)


def solution(mesh):
    return jax.shard_map(
        on_device,
        mesh=mesh,
        in_specs=(
            P("dp", None, None),
            P("dp", None, None),
            P(None, "head"),
            P("head"),
            P(None, "head"),
            P(None, "head"),
            P("head"),
            P("head", None),
            P(),
            P(),
            P(),
            P(None, "head"),
            P("head"),
            P("head", None),
            P(),
            P(),
            P(),
            P("dp", None),
            P("dp", None, None),
        ),
        out_specs=(
            P("dp", "head", None),
            P("dp", "head", None),
            P("dp", "head", None),
            P("dp", "head", None),
            P(None, "head"),
            P("head"),
            P(None, "head"),
            P(None, "head"),
            P("head"),
            P("head", None),
            P(),
            P(),
            P(),
            P(None, "head"),
            P("head"),
            P("head", None),
            P(),
            P(),
            P(),
        ),
        check_vma=False,
    )
```

```python
import math

import jax
import jax.numpy as jnp
from jax import lax
from jax.experimental import pallas as pl
from jax.experimental.pallas import tpu as pltpu
from jax.sharding import PartitionSpec as P

HDIM = 64
GROUP = 16
MESH = pl.DeviceIdType.MESH

norm_eps = 1e-12
root_half = 1.0 / math.sqrt(2.0)
gauss_norm = 1.0 / math.sqrt(2.0 * math.pi)
low_type = jnp.bfloat16
full_type = jnp.float32


def norm_stats(values):
    center = values - jnp.mean(values, axis=-1, keepdims=True)
    inverse = lax.rsqrt(jnp.mean(center * center, axis=-1, keepdims=True) + norm_eps)
    return center * inverse, inverse


def norm_backward(upstream, scaled, inverse, gain_vector):
    weighted = upstream * gain_vector
    plain_mean = jnp.mean(weighted, axis=-1, keepdims=True)
    cross_mean = jnp.mean(weighted * scaled, axis=-1, keepdims=True)
    return inverse * (weighted - plain_mean - scaled * cross_mean)


class Place:
    def __init__(self):
        index = lax.axis_index("dp")
        self.head = lax.axis_index("head")
        base = index // GROUP * GROUP
        inner = lax.rem(index, GROUP)
        self.x = lax.rem(inner, 2)
        self.y = lax.rem(inner // 2, 2)
        self.z = inner // 4
        self.base = base
        self.twin = (index, 1 - self.head)

    def at(self, x, y, z):
        return (self.base + z * 4 + y * 2 + x, self.head)

    def axes(self, flip):
        x_next = self.at(1 - self.x, self.y, self.z)
        y_next = self.at(self.x, 1 - self.y, self.z)
        if flip:
            return self.y, self.x, y_next, x_next
        return self.x, self.y, x_next, y_next

    def z_plus(self, step):
        return lax.rem(self.z + step, 4)

    def along_z(self, step):
        return self.at(self.x, self.y, self.z_plus(step))

    def partners(self):
        found = [self.twin, self.at(1 - self.x, self.y, self.z), self.at(self.x, 1 - self.y, self.z)]
        return found + [self.along_z(step) for step in (1, 2, 3)]


def remote(src, dst, send, recv, device):
    return pltpu.make_async_remote_copy(
        src_ref=src, dst_ref=dst, send_sem=send, recv_sem=recv, device_id=device, device_id_type=MESH
    )


AXES = ("xyz", "zxy", "xyz", "yzx")
PLAN = {
    "query": ("F1", "F2", "z1"),
    "kv": ("s1",),
    "rows1": ("F3", "z2", "r02"),
    "pair1": ("s2",),
    "pair2": ("r22", "r32"),
    "pair4": ("r03",),
    "pair5": ("z3",),
    "norm1": ("s3",),
    "ff00": ("r23", "r12"),
    "ff02": ("r33",),
    "ff10": ("p",),
    "ff12": ("r13",),
    "last1": ("r04", "q0"),
    "mid0": ("r24",),
    "mid1": ("r34", "r14"),
    "mid2": ("r05", "r25"),
    "to3": ("q1",),
    "mid3": ("r35", "r15"),
    "wide0": ("r06", "r26"),
    "wide1": ("r36", "r16"),
}


class Reduce:
    def __init__(self, place, slot, src_ref, out_ref, inbox, send, recv):
        self.place, self.slot, self.axes = place, slot, AXES[slot]
        self.src, self.out, self.inbox = src_ref, out_ref, inbox
        self.send, self.recv = send, recv
        self.count = self.fill = 0
        self.last = []
        self.copies = []
        self.spans = [(0, src_ref.shape[0])]

    def others(self, axis):
        place = self.place
        if axis == "z":
            return [(place.z_plus(step), step - 1, place.along_z(step)) for step in (1, 3, 2)]
        low_bit, high_bit = lax.rem(place.z, 2), place.z // 2
        if axis == "x":
            return [(1 - place.x, 0, place.at(1 - place.x, place.y, place.z))]
        if axis == "y":
            return [(1 - place.y, 0, place.at(place.x, 1 - place.y, place.z))]
        if axis == "l":
            return [(1 - low_bit, 0, place.at(place.x, place.y, place.z + 1 - 2 * low_bit))]
        return [(1 - high_bit, 0, place.at(place.x, place.y, place.z + 2 - 4 * high_bit))]

    def part(self, axis):
        place = self.place
        return {"x": place.x, "y": place.y, "z": place.z, "l": lax.rem(place.z, 2), "h": place.z // 2}[axis]

    def put(self, src, dst, device):
        copy = remote(src, dst, self.send.at[self.slot, self.count], self.recv.at[self.slot, self.count], device)
        copy.start()
        self.count += 1
        self.last.append(copy)
        self.copies.append(copy)

    def landed(self):
        for copy in self.last:
            copy.wait_recv()
        self.last = []

    def step(self, number):
        depth = len(self.axes)
        if number <= depth:
            if number > 1:
                self.add()
            axis = self.axes[number - 1]
            start, size = self.spans[-1]
            others = self.others(axis)
            rows = size // (len(others) + 1)
            for part, slot, device in others:
                into = self.inbox.at[pl.ds(self.fill + slot * rows, rows)]
                self.put(self.src.at[at_rows(start + part * rows, rows)], into, device)
            self.pending = (self.fill, len(others), rows)
            self.fill += len(others) * rows
            self.spans.append((start + self.part(axis) * rows, rows))
        else:
            if number == depth + 1:
                self.add()
            else:
                self.landed()
            start, rows = self.spans[2 * depth + 1 - number]
            mine = at_rows(start, rows)
            for _, _, device in self.others(self.axes[2 * depth - number]):
                self.put(self.out.at[mine], self.out.at[mine], device)

    def add(self):
        self.landed()
        fill, count, rows = self.pending
        mine = at_rows(self.spans[-1][0], rows)
        total = self.src[mine].astype(full_type)
        for slot in range(count):
            total += self.inbox[pl.ds(fill + slot * rows, rows)].astype(full_type)
        target = self.out if len(self.spans) > len(self.axes) else self.src
        target[mine] = total.astype(low_type)

    def finish(self):
        self.landed()
        for copy in self.copies:
            copy.wait_send()


class SmallGather:
    def __init__(self, place, all_ref, send, recv):
        self.place, self.all, self.send, self.recv = place, all_ref, send, recv
        self.line = (place.y * 2 + place.x) * 4
        self.copies = []

    def put(self, start, count, device):
        ref = self.all.at[pl.ds(start, count)]
        slot = len(self.copies)
        copy = remote(ref, ref, self.send.at[slot], self.recv.at[slot], device)
        copy.start()
        self.copies.append(copy)

    def step_1(self):
        for step in (1, 2, 3):
            self.put(self.line + self.place.z, 1, self.place.along_z(step))

    def step_2(self):
        for step in (1, 2, 3):
            ref = self.all.at[pl.ds(self.line + self.place.z_plus(step), 1)]
            remote(ref, ref, self.send.at[0], self.recv.at[3 - step], self.place.along_z(step)).wait_recv()
        self.put(self.line, 4, self.place.at(1 - self.place.x, self.place.y, self.place.z))

    def step_3(self):
        self.copies[3].wait_recv()
        self.put(self.place.y * 8, 8, self.place.at(self.place.x, 1 - self.place.y, self.place.z))

    def finish(self):
        self.copies[4].wait_recv()
        for copy in self.copies:
            copy.wait_send()


def dots(left, right, left_dim=1, right_dim=0):
    return lax.dot_general(
        left, right, (((left_dim,), (right_dim,)), ((), ())), preferred_element_type=full_type
    )


def at_rows(start, count):
    return pl.ds(pl.multiple_of(start, 16), count)


def lanes(index, count):
    return pl.ds(pl.multiple_of(index * count, count), count)


def repeat(count, body):
    def step(index, carry):
        body(index)
        return carry

    lax.fori_loop(0, count, step, 0)


class Gather:
    def __init__(self, place, all_ref, half, send, recv, twin_recv):
        self.place, self.all, self.half = place, all_ref, half
        self.size = all_ref.shape[1] // (2 * GROUP)
        self.send, self.recv, self.twin_recv = send, recv, twin_recv
        self.p, self.q, self.p_next, self.q_next = place.axes(half == 1)
        self.own = self.block(self.q, self.p, place.z)
        self.sends = []
        z = place.z
        far = z // 2
        self.z_from = (z, 1 - z + 4 * far, 2 - far, 3 - 3 * far)
        inward, outward = 1 + lax.rem(z, 2), lax.rem(3 * z - 3 + 12, 12)
        self.inward, self.outward = place.at(place.x, place.y, inward), place.at(place.x, place.y, outward)
        across = place.at(place.x, place.y, 3 - z)
        self.z_next = (None, across, self.outward, self.outward)
        self.between = lax.rem(z, 3) != 0

    def block(self, q, p, z):
        return (q * 2 + p) * 4 + z

    def rows(self, block):
        return at_rows((self.half * GROUP + block) * self.size, self.size)

    def ref(self, block, kind):
        return self.all.at[kind, self.rows(block)]

    def pass_on(self, block, device, only=None):
        slot = len(self.sends)

        def copy():
            ref = self.ref(block, self.place.head)
            return remote(ref, ref, self.send.at[self.half, slot], self.recv.at[self.half, block], device)

        self.sends.append((copy, only))
        if only is None:
            copy().start()
        else:
            pl.when(only)(lambda: copy().start())

    def to_twin(self, block):
        slot = len(self.sends)

        def copy():
            ref = self.ref(block, self.place.head)
            return remote(ref, ref, self.send.at[self.half, slot], self.twin_recv.at[self.half, block], self.place.twin)

        self.sends.append((copy, None))
        copy().start()

    def landed(self, block):
        ref = self.ref(block, self.place.head)
        remote(ref, ref, self.send.at[self.half, 0], self.recv.at[self.half, block], self.p_next).wait_recv()

    def start(self):
        self.sends.clear()
        self.pass_on(self.own, self.inward)
        self.pass_on(self.own, self.outward, self.between)
        self.pass_on(self.own, self.p_next)

    def plane(self, side, other):
        q = self.q if side == 0 else 1 - self.q
        p = self.p if other == 0 else 1 - self.p
        return at_rows((self.half * GROUP + self.block(q, p, 0)) * self.size, 4 * self.size)

    def plane_copy(self, side, other, kind, slot, recv, device):
        ref = self.all.at[kind, self.plane(side, other)]
        return remote(ref, ref, self.send.at[self.half, slot], recv.at[self.half, GROUP + side * 2 + other], device)

    def plane_on(self, side, other, recv, device, lands=None):
        slot = len(self.sends)
        ref = self.all.at[self.place.head, self.plane(side, other)]
        side, other = (side, other) if lands is None else lands

        def copy():
            there = recv.at[self.half, GROUP + side * 2 + other]
            return remote(ref, ref, self.send.at[self.half, slot], there, device)

        self.sends.append((copy, None))
        copy().start()

    def forward(self, step):
        block = self.block(self.q, self.p, self.z_from[step])
        pl.when(self.between)(lambda: self.landed(block))
        self.pass_on(block, self.z_next[step], self.between)

    def z_step(self, step):
        block = self.block(self.q, self.p, self.z_from[step])
        pl.when(jnp.logical_not(self.between))(lambda: self.landed(block))
        self.pass_on(block, self.p_next)
        self.to_twin(block)
        if step == 3:
            self.plane_on(0, 0, self.recv, self.q_next, (1, 0))

    def p_step(self):
        for step in range(4):
            self.landed(self.block(self.q, 1 - self.p, self.z_from[step]))
        self.plane_on(0, 1, self.recv, self.q_next, (1, 1))
        self.plane_on(0, 1, self.twin_recv, self.place.twin)

    def q_step(self, other):
        self.plane_copy(1, other, self.place.head, 0, self.recv, self.q_next).wait_recv()
        self.plane_on(1, other, self.twin_recv, self.place.twin)

    def plane_landed(self, side, other):
        kind = 1 - self.place.head
        if side + other > 0:
            self.plane_copy(side, other, kind, 0, self.twin_recv, self.place.twin).wait_recv()
            return
        for step in range(1, 4):
            block = self.block(self.q, self.p, self.z_from[step])
            ref = self.ref(block, kind)
            remote(
                ref, ref, self.send.at[self.half, 0], self.twin_recv.at[self.half, block], self.place.twin
            ).wait_recv()

    def finish(self):
        for copy, only in self.sends:
            if only is None:
                copy().wait_send()
            else:
                pl.when(only)(lambda copy=copy: copy().wait_send())


def layer_kernel(
    tokens_any, query_any, key_any, value_any, out_any, inner_any, outer_any,
    memory_ref, index_ref, cot_ref, query_bias_ref, value_bias_ref, out_bias_ref, first_gain_ref, first_shift_ref,
    inner_bias_ref, outer_bias_ref, second_gain_ref, second_shift_ref,
    layer_any, memory_out_any, tokens_grad_any, memory_grad_any, sum_any, outer_grad_any, inner_grad_any, vec_any,
    rows, wq, wkv, wo, wi, wu, load_sem,
    pick, keys, values, pair_values, rows_m, query_m, probs, context_m, swap_out, swap_in,
    first_scaled, fig, slope, query_grad, kv_grad, spread, stage,
    all_ref, small_all, grads, inbox,
    part_t, got_t, query_d, context_d, normed_d, pool,
    g_send, g_recv, t_recv, r_send, r_recv, s_send, s_recv, x_send, x_recv,
    layer_out_ref, memory_out_ref, tokens_grad_ref, memory_grad_ref, sum_ref, outer_grad_ref, inner_grad_ref,
    vec_out_ref, store_sem,
):
    segs, seq, width = tokens_any.shape
    mem_len = memory_ref.shape[0]
    mem_pad = -(-mem_len // 32) * 32
    tall = seq + mem_pad
    masked = cot_ref.shape[1]
    m_rows = segs * masked
    own_seq = seq // 2
    own = own_seq + mem_pad
    half = query_any.shape[1]
    pairs = half // 128
    key_rows = keys.shape[1]
    hidden = inner_any.shape[1]
    place = Place()
    head = place.head
    gate = lax.broadcasted_iota(jnp.int32, (1, 128), 1) < HDIM
    score_scale = 1.0 / math.sqrt(HDIM)

    loads = []

    def load(src, dst):
        copy = pltpu.make_async_copy(src, dst, load_sem.at[len(loads)])
        copy.start()
        loads.append(copy)
        return copy

    stores = []

    def store(src, dst):
        copy = pltpu.make_async_copy(src, dst, store_sem.at[len(stores)])
        copy.start()
        stores.append(copy)

    load_rows = []
    for s in range(segs):
        load_rows.append(load(tokens_any.at[s], rows.at[pl.ds(s * tall, seq)]))
    load_kv = [load(key_any, wkv.at[:, pl.ds(0, half)]), load(value_any, wkv.at[:, pl.ds(half, half)])]
    load_q, load_o = load(query_any, wq), load(out_any, wo)
    load_i, load_u = load(inner_any, wi), load(outer_any, wu)

    barrier = pltpu.get_barrier_semaphore()
    partners = place.partners()
    for partner in partners:
        pl.semaphore_signal(barrier, inc=1, device_id=partner, device_id_type=MESH)

    def vector(ref, start=0, count=None):
        count = ref.shape[0] if count is None else count
        return ref[pl.ds(start, count)].astype(full_type).reshape(1, count)

    out_bias, first_gain, first_shift = vector(out_bias_ref), vector(first_gain_ref), vector(first_shift_ref)
    outer_bias, second_gain, second_shift = vector(outer_bias_ref), vector(second_gain_ref), vector(second_shift_ref)
    query_bias, value_bias = vector(query_bias_ref), vector(value_bias_ref)
    key_index = lax.broadcasted_iota(jnp.int32, (1, key_rows - seq), 1)
    key_mask = jnp.where(key_index < mem_len, 0.0, -1e30).astype(full_type)

    def inner_bias(part):
        return vector(inner_bias_ref, part * width, width)

    memory = memory_ref[...].astype(full_type)
    blank = jnp.zeros((mem_pad - mem_len, width), full_type)
    for s in range(segs):
        filled = jnp.concatenate([memory[:, s, :], blank], axis=0)
        rows[pl.ds(s * tall + seq, mem_pad)] = filled.astype(low_type)
    keys[:, pl.ds(tall, key_rows - tall)] = jnp.zeros((segs, key_rows - tall, half), low_type)
    values[:, pl.ds(tall, key_rows - tall)] = jnp.zeros((segs, key_rows - tall, half), low_type)
    for s in range(segs):
        hot = index_ref[s : s + 1] == lax.broadcasted_iota(jnp.int32, (seq, masked), 0)
        pick[s] = jnp.where(hot, 1.0, 0.0).astype(low_type)

    for copy in load_rows + load_kv:
        copy.wait()

    def key_value(s):
        both = dots(rows[at_rows(s * tall, tall)], wkv[...])
        keys[s, 0:tall] = both[:, :half].astype(low_type)
        values[s, 0:tall] = (both[:, half:] + value_bias).astype(low_type)

    repeat(segs, key_value)

    load_q.wait()
    for s in range(segs):
        m = pl.ds(s * masked, masked)
        found = dots(pick[s], rows[pl.ds(s * tall, seq)], 0, 0).astype(low_type)
        rows_m[m] = found
    query_m[...] = (dots(rows_m[...], wq[...]) + query_bias).astype(low_type)

    def apart(pair):
        zero = jnp.zeros_like(pair)
        return jnp.concatenate([jnp.where(gate, pair, zero), jnp.where(gate, zero, pair)], axis=0)

    def masked_attention(i):
        s, pair = i // pairs, lax.rem(i, pairs)
        m, cols = at_rows(s * masked, masked), lanes(pair, 128)
        scores = dots(apart(query_m[m, cols]), keys[s, :, cols], 1, 1) * score_scale
        scores = jnp.concatenate([scores[:, :seq], scores[:, seq:] + key_mask], axis=1)
        raised = jnp.exp(scores - jnp.max(scores, axis=1, keepdims=True))
        share = raised / jnp.sum(raised, axis=1, keepdims=True)
        probs[i] = share
        found = dots(share.astype(low_type), values[s, :, cols])
        context_m[m, cols] = jnp.where(gate, found[:masked], found[masked:]).astype(low_type)

    repeat(segs * pairs, masked_attention)

    exchanges = []

    def twin_copy(src, dst):
        slot = len(exchanges)
        copy = remote(src, dst, x_send.at[slot], x_recv.at[slot], place.twin)
        copy.start()
        exchanges.append(copy)
        return copy

    def swap(slot, partial):
        swap_out[slot] = partial.astype(low_type)
        return twin_copy(swap_out.at[slot], swap_in.at[slot])

    def swapped(slot, copy):
        copy.wait_recv()
        return swap_out[slot].astype(full_type) + swap_in[slot].astype(full_type)

    load_o.wait()
    partial = dots(context_m[...], wo[...])
    pl.semaphore_wait(barrier, len(partners))
    swapping = swap(0, partial)

    def spread_values(i):
        s, pair = i // pairs, lax.rem(i, pairs)
        v = values[s, :, lanes(pair, 128)]
        ones = jnp.ones_like(v)
        pair_values[i, 0] = jnp.where(gate, v, ones)
        pair_values[i, 1] = jnp.where(gate, ones, v)

    repeat(segs * pairs, spread_values)

    load_i.wait()
    load_u.wait()
    scaled, inverse = norm_stats(rows_m[...].astype(full_type) + (swapped(0, swapping) + out_bias))
    first_scaled[...] = scaled
    normed = scaled * first_gain + first_shift
    normed_low = normed.astype(low_type)
    gathers = [Gather(place, all_ref, part, g_send, g_recv, t_recv) for part in range(2)]
    for part, gather in enumerate(gathers):
        all_ref[0, gather.rows(gather.own)] = normed_low[part * masked : (part + 1) * masked]
    @pl.when(head == 0)
    def _():
        for gather in gathers:
            gather.start()

    partial = jnp.zeros((m_rows, width), full_type)
    parts = hidden // width
    for part in range(parts):
        cols = slice(part * width, (part + 1) * width)
        pre_act = dots(normed_low, wi[:, cols]) + inner_bias(part)
        share = 0.5 * (1.0 + lax.erf(pre_act * root_half))
        slope[:, cols] = share + pre_act * jnp.exp(-0.5 * pre_act * pre_act) * gauss_norm
        partial += dots((pre_act * share).astype(low_type), wu[cols])
    swapping = swap(1, partial)
    scaled2, inverse2 = norm_stats(normed + (swapped(1, swapping) + outer_bias))
    upstream = cot_ref[...].reshape(m_rows, width).astype(full_type)
    second_in_grad = norm_backward(upstream, scaled2, inverse2, second_gain)
    outer_grad = second_in_grad.astype(low_type)
    for part, gather in enumerate(gathers):
        all_ref[1, gather.rows(gather.own)] = outer_grad[part * masked : (part + 1) * masked]

    @pl.when(head == 1)
    def _():
        for gather in gathers:
            gather.start()

    small = SmallGather(place, small_all, s_send, s_recv)
    mine = small.line + place.z
    reduces = [
        Reduce(place, slot, grads.at[slot], sum_ref.at[slot], inbox.at[slot], r_send, r_recv) for slot in range(4)
    ]

    def tick(name):
        for event in PLAN.get(name, ()):
            if event[0] == "r":
                reduces[int(event[1])].step(int(event[2]))
            elif event[0] == "s":
                getattr(small, "step_" + event[1])()
            else:
                for gather in gathers:
                    if event[0] == "F":
                        gather.forward(int(event[1]))
                    elif event[0] == "z":
                        gather.z_step(int(event[1]))
                    elif event[0] == "p":
                        gather.p_step()
                    else:
                        gather.q_step(int(event[1]))

    def column_sum(value):
        return jnp.sum(value, axis=0, keepdims=True)

    second_gain_part, second_shift_part = column_sum(upstream * scaled2), column_sum(upstream)

    partial = jnp.zeros((m_rows, width), full_type)
    for part in range(parts):
        cols = slice(part * width, (part + 1) * width)
        inner_grad = (dots(outer_grad, wu[cols], 1, 1) * slope[:, cols]).astype(low_type)
        partial += dots(inner_grad, wi[:, cols], 1, 1)
    swapping = swap(2, partial)
    tick("swap")
    normed_grad = second_in_grad + swapped(2, swapping)
    scaled = first_scaled[...]
    first_in_grad = norm_backward(normed_grad, scaled, inverse, first_gain)
    fig[...] = first_in_grad
    attention_grad = first_in_grad.astype(low_type)
    small_all[mine, 0:1] = column_sum(attention_grad.astype(full_type))
    small_all[mine, 1:2] = column_sum(normed_grad * scaled)
    small_all[mine, 2:3] = column_sum(normed_grad)
    small_all[mine, 3:4] = second_gain_part
    small_all[mine, 4:5] = second_shift_part
    out_grad = dots(context_m[...], attention_grad, 0, 0).astype(low_type)
    grads[0, 0:half] = out_grad[:, :half]
    grads[0, half : 2 * half] = out_grad[:, half:]
    reduces[0].step(1)
    stage[...] = dots(attention_grad, wo[...], 1, 1).astype(low_type)

    def masked_back(i):
        s, pair = i // pairs, lax.rem(i, pairs)
        m, cols = at_rows(s * masked, masked), lanes(pair, 128)
        value_cols = pl.ds(pl.multiple_of(half + pair * 128, 128), 128)
        context_grad = apart(stage[m, cols])
        share = probs[i]
        weighed = share * dots(context_grad, values[s, :, cols], 1, 1)
        score_grad = (weighed - share * jnp.sum(weighed, axis=1, keepdims=True)).astype(low_type)
        all_rows = at_rows(s * tall, tall)
        found = dots(share.astype(low_type), context_grad, 0, 0)
        kv_grad[all_rows, value_cols] = found[:tall].astype(low_type)
        found = dots(score_grad, apart(query_m[m, cols]), 0, 0) * score_scale
        kv_grad[all_rows, cols] = found[:tall].astype(low_type)
        found = dots(score_grad, keys[s, :, cols]) * score_scale
        query_grad[m, cols] = jnp.where(gate, found[:masked], found[masked:]).astype(low_type)

    repeat(segs * pairs, masked_back)
    tick("back")
    grads[1] = dots(rows_m[...], query_grad[...], 0, 0).astype(low_type)
    small_all[mine, 5:6] = jnp.concatenate(
        [
            column_sum(query_grad[...].astype(full_type)),
            column_sum(kv_grad[:, half:].astype(full_type)),
        ],
        axis=1,
    )
    small_all[mine, 6:8] = jnp.zeros((2, width), full_type)
    tick("query")

    def key_value_grad(c):
        cols = lanes(c, 256)
        found = dots(rows[:, cols], kv_grad[...], 0, 0).astype(low_type)
        grads[2, cols] = found[:, :half]
        grads[3, cols] = found[:, half:]

    repeat(width // 256, key_value_grad)
    reduces[2].step(1)
    reduces[3].step(1)
    tick("kv")

    masked_part = dots(query_grad[...], wq[...], 1, 1) + jnp.where(head == 0, fig[...], 0.0)
    high = masked_part.astype(low_type)
    rest = (masked_part - high.astype(full_type)).astype(low_type)
    for s in range(segs):
        spread[s, 0:masked] = high[s * masked : (s + 1) * masked]
        spread[s, masked : 2 * masked] = rest[s * masked : (s + 1) * masked]

    def row_grad(i):
        s, c = i // 2, lax.rem(i, 2)
        here = at_rows(s * tall + c * own_seq, own_seq)
        found = dots(kv_grad[here], wkv[...], 1, 1)
        chosen = pick[s, at_rows(c * own_seq, own_seq)]
        found += dots(chosen, spread[s, 0:masked]) + dots(chosen, spread[s, masked : 2 * masked])
        part_t[here] = found.astype(low_type)

    repeat(segs, row_grad)
    tick("rows0")
    repeat(segs, lambda i: row_grad(i + segs))
    for s in range(segs):
        here = pl.ds(s * tall + seq, mem_pad)
        part_t[here] = dots(kv_grad[here], wkv[...], 1, 1).astype(low_type)

    def send_rows(source, target, s):
        away = at_rows(s * tall + (1 - head) * own_seq, own_seq)
        one = twin_copy(source.at[away], target.at[pl.ds(s * own, own_seq)])
        two = twin_copy(source.at[pl.ds(s * tall + seq, mem_pad)], target.at[pl.ds(s * own + own_seq, mem_pad)])
        return one, two

    moved_t = [send_rows(part_t, got_t, s) for s in range(segs)]
    tick("rows1")
    reduces[1].step(1)

    pool_at = 0

    def region(count):
        nonlocal pool_at
        pool_at += count
        return pool.at[pl.ds(pool_at - count, count)]

    part_a, got_a, low_d = region(segs * tall), region(segs * own), region(segs * tall)
    part_f, got_f = region(segs * tall), region(segs * own)
    active = region(parts * tall)

    def dense_query(s):
        here = at_rows(s * tall, tall)
        query_d[here] = (dots(rows[here], wq[...]) + query_bias).astype(low_type)

    repeat(segs, dense_query)
    exp_scale = score_scale * math.log2(math.e)

    def dense_attention(s, pair):
        cols = lanes(pair, 128)
        block_rows = tall // 2
        k = keys[s, :, cols]
        for block in range(2):
            here = at_rows(s * tall + block * block_rows, block_rows)
            query = query_d[here, cols]
            zero = jnp.zeros_like(query)
            found = []
            for side in range(2):
                lone = jnp.where(gate, query, zero) if side == 0 else jnp.where(gate, zero, query)
                scores = dots(lone, k, 1, 1)
                scores = jnp.concatenate([scores[:, :seq], scores[:, seq:] + key_mask], axis=1)
                raised = jnp.exp2((scores - jnp.max(scores, axis=1, keepdims=True)) * exp_scale)
                found.append(dots(raised.astype(low_type), pair_values[s * pairs + pair, side]))
            top = jnp.where(gate, found[0], found[1])
            total = pltpu.roll(jnp.where(gate, found[1], found[0]), HDIM, 1)
            context_d[here, cols] = (top / total).astype(low_type)

    def dense_out(s):
        here = pl.ds(s * tall, tall)
        part_a[here] = dots(context_d[here], wo[...]).astype(low_type)

    def norm_first(s, local, count):
        tokens_here = at_rows(s * tall + head * own_seq + local, count)
        here = pl.ds(s * tall + seq, count) if local == own_seq else tokens_here
        near = pl.ds(s * own + local, count)
        total = part_a[here].astype(full_type) + got_a[near].astype(full_type) + out_bias
        scaled, _ = norm_stats(rows[here].astype(full_type) + total)
        value = scaled * first_gain + first_shift
        normed_d[near] = value
        low_d[here] = value.astype(low_type)

    def norm_second(s, local, count):
        tokens_here = at_rows(s * tall + head * own_seq + local, count)
        here = pl.ds(s * tall + seq, count) if local == own_seq else tokens_here
        near = pl.ds(s * own + local, count)
        total = part_f[here].astype(full_type) + got_f[near].astype(full_type) + outer_bias
        scaled, _ = norm_stats(normed_d[near] + total)
        value = (scaled * second_gain + second_shift).astype(low_type)
        if local == own_seq:
            memory_out_ref[s] = value
        else:
            layer_out_ref[s, pl.ds(local, count)] = value

    chunk = 128
    spans = [(c * chunk, chunk) for c in range(own_seq // chunk)] + [(own_seq, mem_pad)]
    moved_a = []
    for s in range(segs):
        for pair in range(pairs):
            dense_attention(s, pair)
            tick("pair%d" % (s * pairs + pair))
        dense_out(s)
        moved_a.append(send_rows(part_a, got_a, s))
        tick("out%d" % s)
    moved_n = []
    for s in range(segs):
        for copy in moved_a[s]:
            copy.wait_recv()
        for local, count in spans:
            norm_first(s, local, count)
        ours = low_d.at[at_rows(s * tall + head * own_seq, own_seq)]
        moved_n.append(twin_copy(ours, ours))
        tick("norm%d" % s)
    for s in range(segs):
        for copy in moved_t[s]:
            copy.wait_recv()
        ours = at_rows(s * tall + head * own_seq, own_seq)
        near = got_t[pl.ds(s * own, own_seq)].astype(full_type)
        tokens_grad_ref[s] = (part_t[ours].astype(full_type) + near).astype(low_type)
        near = got_t[pl.ds(s * own + own_seq, mem_pad)].astype(full_type)
        memory_grad_ref[s] = (part_t[pl.ds(s * tall + seq, mem_pad)].astype(full_type) + near).astype(low_type)
    store(tokens_grad_ref, tokens_grad_any)
    store(memory_grad_ref, memory_grad_any)
    moved_f = []
    for s in range(segs):
        moved_n[s].wait_recv()
        here = pl.ds(s * tall, tall)
        for part in range(parts):
            cols = slice(part * width, (part + 1) * width)
            pre_act = dots(low_d[here], wi[:, cols]) + inner_bias(part)
            active[pl.ds(part * tall, tall)] = (0.5 * pre_act * (1.0 + lax.erf(pre_act * root_half))).astype(low_type)
            tick("ff%d%d" % (s, part))
        partial = dots(active[pl.ds(0, tall)], wu[0:width])
        for part in range(1, parts):
            partial += dots(active[pl.ds(part * tall, tall)], wu[part * width : (part + 1) * width])
        part_f[here] = partial.astype(low_type)
        moved_f.append(send_rows(part_f, got_f, s))
        tick("ff%d2" % s)
    for s in range(segs):
        for copy in moved_f[s]:
            copy.wait_recv()
        for local, count in spans:
            norm_second(s, local, count)
        tick("last%d" % s)
    store(layer_out_ref, layer_any)
    store(memory_out_ref, memory_out_any)
    for copy in exchanges:
        copy.wait_send()

    total_rows = all_ref.shape[1]
    active_all, inner_grad_all = pool.at[pl.ds(0, total_rows)], pool.at[pl.ds(total_rows, total_rows)]
    ones = jnp.ones((16, total_rows), low_type)

    def hidden_block(part, here):
        cols = slice(part * width, (part + 1) * width)
        pre_act = dots(all_ref[0, here], wi[:, cols]) + inner_bias(part)
        back = dots(all_ref[1, here], wu[cols], 1, 1)
        share = 0.5 * (1.0 + lax.erf(pre_act * root_half))
        active_all[here] = (pre_act * share).astype(low_type)
        bell = pre_act * jnp.exp(-0.5 * pre_act * pre_act) * gauss_norm
        inner_grad_all[here] = (back * (share + bell)).astype(low_type)

    blocks = 4
    block_rows = total_rows // blocks
    for part in range(parts):
        cols = slice(part * width, (part + 1) * width)
        if part == 0:
            for group, (side, other) in enumerate(((0, 0), (0, 1), (1, 0), (1, 1))):
                tick("to%d" % group)
                for gather in gathers:
                    gather.plane_landed(side, other)
                starts = [gather.plane(side, other).start for gather in gathers]

                def both_halves(i):
                    start = starts[0] * (1 - i) + starts[1] * i
                    hidden_block(0, at_rows(start, total_rows // 8))

                repeat(2, both_halves)
                tick("mid%d" % group)
        else:
            repeat(blocks // 2, lambda i: hidden_block(part, at_rows(i * block_rows, block_rows)))
            tick("half%d" % part)
            repeat(blocks // 2, lambda i: hidden_block(part, at_rows((i + blocks // 2) * block_rows, block_rows)))
            tick("wide%d" % (3 * part - 1))
        outer_grad_ref[cols] = dots(active_all[...], all_ref[1], 0, 0).astype(low_type)
        store(outer_grad_ref.at[cols], outer_grad_any.at[cols])
        tick("wide%d" % (3 * part))
        inner_grad_ref[:, cols] = dots(all_ref[0], inner_grad_all[...], 0, 0).astype(low_type)
        store(inner_grad_ref.at[:, cols], inner_grad_any.at[:, cols])
        vec_out_ref[8 + part : 9 + part] = dots(ones, inner_grad_all[...])[0:1]
        tick("wide%d" % (3 * part + 1))
    vec_out_ref[10:11] = dots(ones, all_ref[1])[0:1]
    small.finish()
    total = small_all[0]
    for block in range(1, GROUP):
        total += small_all[block]
    vec_out_ref[0:8] = total
    vec_out_ref[11:16] = jnp.zeros((5, width), full_type)
    store(vec_out_ref, vec_any)
    for slot, reduce in enumerate(reduces):
        reduce.finish()
        store(sum_ref.at[slot], sum_any.at[slot])
    for gather in gathers:
        gather.finish()
    for copy in stores:
        copy.wait()


def layer(tokens, memory, weights, index, cotangent, vectors):
    segs, seq, width = tokens.shape
    mem_pad, masked = -(-memory.shape[0] // 32) * 32, cotangent.shape[1]
    half, hidden = weights[0].shape[1], weights[4].shape[1]
    tall, own, m_rows = seq + mem_pad, seq // 2 + mem_pad, segs * masked
    key_rows = -(-tall // 128) * 128
    pairs, parts = half // 128, hidden // width
    total_rows = GROUP * m_rows
    pool_rows = max(2 * total_rows, (3 * segs + parts) * tall + 2 * segs * own)
    vmem, anywhere = pl.BlockSpec(memory_space=pltpu.VMEM), pl.BlockSpec(memory_space=pl.ANY)

    def low(*shape):
        return pltpu.VMEM(shape, low_type)

    def full(*shape):
        return pltpu.VMEM(shape, full_type)

    def result(*shape):
        return jax.ShapeDtypeStruct(shape, low_type)

    sems = pltpu.SemaphoreType.DMA
    return pl.pallas_call(
        layer_kernel,
        out_shape=(
            result(segs, seq // 2, width),
            result(segs, mem_pad, width),
            result(segs, seq // 2, width),
            result(segs, mem_pad, width),
            result(4, width, half),
            result(hidden, width),
            result(width, hidden),
            jax.ShapeDtypeStruct((16, width), full_type),
        ),
        in_specs=[anywhere] * 7 + [vmem] * (3 + len(vectors)),
        out_specs=(anywhere,) * 8,
        scratch_shapes=[
            low(segs * tall, width), low(width, half), low(width, 2 * half), low(half, width),
            low(width, hidden), low(hidden, width), sems((segs + 6,)),
            low(segs, seq, masked), low(segs, key_rows, half), low(segs, key_rows, half),
            low(segs * pairs, 2, key_rows, 128), low(m_rows, width), low(m_rows, half),
            full(segs * pairs, 2 * masked, key_rows), low(m_rows, half), low(3, m_rows, width), low(3, m_rows, width),
            full(m_rows, width), full(m_rows, width), full(m_rows, hidden), low(m_rows, half),
            low(segs * tall, 2 * half), low(segs, 2 * masked, width), low(m_rows, half),
            low(2, total_rows, width), full(GROUP, 8, width), low(4, width, half),
            low(4, width - width // GROUP, half),
            low(segs * tall, width), low(segs * own, width), low(segs * tall, half), low(segs * tall, half),
            full(segs * own, width), low(pool_rows, width),
            sems((2, 24)), sems((2, 20)), sems((2, 20)), sems((4, 10)), sems((4, 10)),
            sems((5,)), sems((5,)), sems((3 + 7 * segs,)), sems((3 + 7 * segs,)),
            low(segs, seq // 2, width), low(segs, mem_pad, width), low(segs, seq // 2, width), low(segs, mem_pad, width),
            low(4, width, half), low(hidden, width), low(width, hidden), full(16, width), sems((9 + 2 * parts,)),
        ],
        compiler_params=pltpu.CompilerParams(
            collective_id=0, has_side_effects=True, vmem_limit_bytes=63 * 2**20
        ),
    )(tokens, *weights, memory, index, cotangent, *vectors)


def result_kernel(
    layer_in, memory_in, tokens_in, memory_grad_in, out_a, out_b, query_in, key_in, value_in, outer_in, inner_in, vecs,
    layer_out, memory_out, tokens_grad, memory_grad, query_grad, query_bias, key_grad, value_grad, value_bias,
    out_grad, out_bias, first_gain, first_shift, inner_grad, inner_bias, outer_grad, outer_bias, second_gain, second_shift,
):
    layer_out[...] = layer_in[...]
    tokens_grad[...] = tokens_in[...]
    half = query_grad.shape[1]
    out_grad[:, :half] = out_a[0].astype(full_type)
    out_grad[:, half:] = out_b[0].astype(full_type)
    query_grad[...] = query_in[0].astype(full_type)
    key_grad[...] = key_in[0].astype(full_type)
    value_grad[...] = value_in[0].astype(full_type)
    inner_grad[...] = inner_in[...].astype(full_type)
    outer_grad[...] = outer_in[...].astype(full_type)

    @pl.when(pl.program_id(0) == 0)
    def _():
        count = memory_out.shape[0]
        upper = lax.axis_index("head") > 0
        for source, target in ((memory_in, memory_out), (memory_grad_in, memory_grad)):
            for s in range(source.shape[0]):
                value = source[s].astype(full_type)
                target[:, s] = jnp.where(upper, value[count : 2 * count], value[:count]).astype(low_type)
        for row, target in enumerate((out_bias, first_gain, first_shift, second_gain, second_shift)):
            target[...] = vecs[row]
        query_bias[...] = vecs[5, :half]
        value_bias[...] = vecs[5, half:]
        width = vecs.shape[1]
        for part in range(inner_bias.shape[0] // width):
            inner_bias[pl.ds(part * width, width)] = vecs[8 + part]
        outer_bias[...] = vecs[10]


def results(layer_out, memory_out, tokens_grad, memory_grad, sums, outer_grad, inner_grad, vecs, own_mem):
    segs, own_seq, width = layer_out.shape
    hidden, half = outer_grad.shape[0], sums.shape[2]
    steps = 8

    def rows_of(shape, dim):
        block = tuple(size // steps if i == dim else size for i, size in enumerate(shape))
        return pl.BlockSpec(block, lambda i: tuple(i if d == dim else 0 for d in range(len(shape))))

    def whole(*shape):
        return pl.BlockSpec(shape, lambda i: (0,) * len(shape))

    def part_of_sums(slot, rows, offset=0):
        return pl.BlockSpec((1, rows, half), lambda i: (slot, i + offset, 0))

    def full(*shape):
        return jax.ShapeDtypeStruct(shape, full_type)

    out_rows = half // steps
    moved = rows_of(layer_out.shape, 1)
    memory_shape = (own_mem, segs, width)
    square, tall, wide, out = (width, half), (hidden, width), (width, hidden), (half, width)
    shapes = (
        jax.ShapeDtypeStruct(layer_out.shape, low_type),
        jax.ShapeDtypeStruct(memory_shape, low_type),
        jax.ShapeDtypeStruct(layer_out.shape, low_type),
        jax.ShapeDtypeStruct(memory_shape, low_type),
        full(*square), full(half), full(*square), full(*square), full(half), full(*out), full(width), full(width),
        full(width), full(*wide), full(hidden), full(*tall), full(width), full(width), full(width),
    )
    specs = tuple(
        moved if i in (0, 2) else rows_of(shape.shape, 0) if len(shape.shape) == 2 else whole(*shape.shape)
        for i, shape in enumerate(shapes)
    )
    return pl.pallas_call(
        result_kernel,
        grid=(steps,),
        out_shape=shapes,
        in_specs=[
            moved, whole(*memory_out.shape), moved, whole(*memory_out.shape),
            part_of_sums(0, out_rows), part_of_sums(0, out_rows, steps),
            part_of_sums(1, width // steps), part_of_sums(2, width // steps), part_of_sums(3, width // steps),
            rows_of(tall, 0), rows_of(wide, 0), whole(*vecs.shape),
        ],
        out_specs=specs,
        compiler_params=pltpu.CompilerParams(vmem_limit_bytes=63 * 2**20),
    )(
        layer_out, memory_out, tokens_grad, memory_grad, sums, sums, sums, sums, sums, outer_grad, inner_grad, vecs
    )


def across_groups(values):
    size = lax.axis_size("dp")
    if size == GROUP:
        return values
    total = moved = values.astype(full_type)
    for _ in range(size // GROUP - 1):
        moved = lax.ppermute(moved, "dp", [(i, (i + GROUP) % size) for i in range(size)])
        total = total + moved
    return total


def on_device(
    tokens,
    memory,
    query_weight,
    query_bias,
    key_weight,
    value_weight,
    value_bias,
    out_weight,
    out_bias,
    first_gain,
    first_shift,
    inner_weight,
    inner_bias,
    outer_weight,
    outer_bias,
    second_gain,
    second_shift,
    masked_rows,
    cotangent,
):
    vectors = (
        query_bias, value_bias, out_bias, first_gain, first_shift, inner_bias, outer_bias, second_gain, second_shift,
    )
    weights = (query_weight, key_weight, value_weight, out_weight, inner_weight, outer_weight)
    rows = layer(tokens, jnp.swapaxes(memory, 0, 1), weights, masked_rows, cotangent, vectors)
    sums = tuple(across_groups(values) for values in rows[4:])
    outputs = list(results(*rows[:4], *sums, memory.shape[1] // 2))
    outputs[1], outputs[3] = jnp.swapaxes(outputs[1], 0, 1), jnp.swapaxes(outputs[3], 0, 1)
    return tuple(outputs)


def solution(mesh):
    return jax.shard_map(
        on_device,
        mesh=mesh,
        in_specs=(
            P("dp", None, None),
            P("dp", None, None),
            P(None, "head"),
            P("head"),
            P(None, "head"),
            P(None, "head"),
            P("head"),
            P("head", None),
            P(),
            P(),
            P(),
            P(None, "head"),
            P("head"),
            P("head", None),
            P(),
            P(),
            P(),
            P("dp", None),
            P("dp", None, None),
        ),
        out_specs=(
            P("dp", "head", None),
            P("dp", "head", None),
            P("dp", "head", None),
            P("dp", "head", None),
            P(None, "head"),
            P("head"),
            P(None, "head"),
            P(None, "head"),
            P("head"),
            P("head", None),
            P(),
            P(),
            P(),
            P(None, "head"),
            P("head"),
            P("head", None),
            P(),
            P(),
            P(),
        ),
        check_vma=False,
    )
```

```python
import math

import jax
import jax.numpy as jnp
from jax import lax
from jax.experimental import pallas as pl
from jax.experimental.pallas import tpu as pltpu
from jax.sharding import PartitionSpec as P

HDIM = 64
GROUP = 16
MESH = pl.DeviceIdType.MESH

norm_eps = 1e-12
root_half = 1.0 / math.sqrt(2.0)
gauss_norm = 1.0 / math.sqrt(2.0 * math.pi)
low_type = jnp.bfloat16
full_type = jnp.float32


def norm_stats(values):
    center = values - jnp.mean(values, axis=-1, keepdims=True)
    inverse = lax.rsqrt(jnp.mean(center * center, axis=-1, keepdims=True) + norm_eps)
    return center * inverse, inverse


def norm_backward(upstream, scaled, inverse, gain_vector):
    weighted = upstream * gain_vector
    plain_mean = jnp.mean(weighted, axis=-1, keepdims=True)
    cross_mean = jnp.mean(weighted * scaled, axis=-1, keepdims=True)
    return inverse * (weighted - plain_mean - scaled * cross_mean)


class Place:
    def __init__(self):
        index = lax.axis_index("dp")
        self.head = lax.axis_index("head")
        base = index // GROUP * GROUP
        inner = lax.rem(index, GROUP)
        self.x = lax.rem(inner, 2)
        self.y = lax.rem(inner // 2, 2)
        self.z = inner // 4
        self.base = base
        self.twin = (index, 1 - self.head)

    def at(self, x, y, z):
        return (self.base + z * 4 + y * 2 + x, self.head)

    def axes(self, flip):
        x_next = self.at(1 - self.x, self.y, self.z)
        y_next = self.at(self.x, 1 - self.y, self.z)
        if flip:
            return self.y, self.x, y_next, x_next
        return self.x, self.y, x_next, y_next

    def z_plus(self, step):
        return lax.rem(self.z + step, 4)

    def along_z(self, step):
        return self.at(self.x, self.y, self.z_plus(step))

    def partners(self):
        found = [self.twin, self.at(1 - self.x, self.y, self.z), self.at(self.x, 1 - self.y, self.z)]
        return found + [self.along_z(step) for step in (1, 2, 3)]


def remote(src, dst, send, recv, device):
    return pltpu.make_async_remote_copy(
        src_ref=src, dst_ref=dst, send_sem=send, recv_sem=recv, device_id=device, device_id_type=MESH
    )


AXES = ("xyz", "zxy", "xyz", "yzx")
PLAN = {
    "query": ("F1", "F2", "z1"),
    "kv": ("s1",),
    "rows1": ("F3", "z2"),
    "pair0": ("r02",),
    "pair1": ("s2",),
    "pair2": ("r22", "r32"),
    "pair4": ("r03",),
    "pair5": ("z3",),
    "norm1": ("s3",),
    "ff00": ("r23", "r12"),
    "ff02": ("r33",),
    "ff10": ("r13",),
    "ff12": ("p",),
    "last1": ("r04",),
    "to2": ("q0",),
    "mid0": ("r24",),
    "mid1": ("r34", "r14"),
    "mid2": ("r05", "r25"),
    "to3": ("q1",),
    "mid3": ("r35", "r15"),
    "wide0": ("r06", "r26"),
    "wide1": ("r36", "r16"),
}


class Reduce:
    def __init__(self, place, slot, src_ref, out_ref, inbox, send, recv):
        self.place, self.slot, self.axes = place, slot, AXES[slot]
        self.src, self.out, self.inbox = src_ref, out_ref, inbox
        self.send, self.recv = send, recv
        self.count = self.fill = 0
        self.last = []
        self.copies = []
        self.spans = [(0, src_ref.shape[0])]

    def others(self, axis):
        place = self.place
        if axis == "z":
            return [(place.z_plus(step), step - 1, place.along_z(step)) for step in (1, 3, 2)]
        low_bit, high_bit = lax.rem(place.z, 2), place.z // 2
        if axis == "x":
            return [(1 - place.x, 0, place.at(1 - place.x, place.y, place.z))]
        if axis == "y":
            return [(1 - place.y, 0, place.at(place.x, 1 - place.y, place.z))]
        if axis == "l":
            return [(1 - low_bit, 0, place.at(place.x, place.y, place.z + 1 - 2 * low_bit))]
        return [(1 - high_bit, 0, place.at(place.x, place.y, place.z + 2 - 4 * high_bit))]

    def part(self, axis):
        place = self.place
        return {"x": place.x, "y": place.y, "z": place.z, "l": lax.rem(place.z, 2), "h": place.z // 2}[axis]

    def put(self, src, dst, device):
        copy = remote(src, dst, self.send.at[self.slot, self.count], self.recv.at[self.slot, self.count], device)
        copy.start()
        self.count += 1
        self.last.append(copy)
        self.copies.append(copy)

    def landed(self):
        for copy in self.last:
            copy.wait_recv()
        self.last = []

    def step(self, number):
        depth = len(self.axes)
        if number <= depth:
            if number > 1:
                self.add()
            axis = self.axes[number - 1]
            start, size = self.spans[-1]
            others = self.others(axis)
            rows = size // (len(others) + 1)
            for part, slot, device in others:
                into = self.inbox.at[pl.ds(self.fill + slot * rows, rows)]
                self.put(self.src.at[at_rows(start + part * rows, rows)], into, device)
            self.pending = (self.fill, len(others), rows)
            self.fill += len(others) * rows
            self.spans.append((start + self.part(axis) * rows, rows))
        else:
            if number == depth + 1:
                self.add()
            else:
                self.landed()
            start, rows = self.spans[2 * depth + 1 - number]
            mine = at_rows(start, rows)
            for _, _, device in self.others(self.axes[2 * depth - number]):
                self.put(self.out.at[mine], self.out.at[mine], device)

    def add(self):
        self.landed()
        fill, count, rows = self.pending
        mine = at_rows(self.spans[-1][0], rows)
        total = self.src[mine].astype(full_type)
        for slot in range(count):
            total += self.inbox[pl.ds(fill + slot * rows, rows)].astype(full_type)
        target = self.out if len(self.spans) > len(self.axes) else self.src
        target[mine] = total.astype(low_type)

    def finish(self):
        self.landed()
        for copy in self.copies:
            copy.wait_send()


class SmallGather:
    def __init__(self, place, all_ref, send, recv):
        self.place, self.all, self.send, self.recv = place, all_ref, send, recv
        self.line = (place.y * 2 + place.x) * 4
        self.copies = []

    def put(self, start, count, device):
        ref = self.all.at[pl.ds(start, count)]
        slot = len(self.copies)
        copy = remote(ref, ref, self.send.at[slot], self.recv.at[slot], device)
        copy.start()
        self.copies.append(copy)

    def step_1(self):
        for step in (1, 2, 3):
            self.put(self.line + self.place.z, 1, self.place.along_z(step))

    def step_2(self):
        for step in (1, 2, 3):
            ref = self.all.at[pl.ds(self.line + self.place.z_plus(step), 1)]
            remote(ref, ref, self.send.at[0], self.recv.at[3 - step], self.place.along_z(step)).wait_recv()
        self.put(self.line, 4, self.place.at(1 - self.place.x, self.place.y, self.place.z))

    def step_3(self):
        self.copies[3].wait_recv()
        self.put(self.place.y * 8, 8, self.place.at(self.place.x, 1 - self.place.y, self.place.z))

    def finish(self):
        self.copies[4].wait_recv()
        for copy in self.copies:
            copy.wait_send()


def dots(left, right, left_dim=1, right_dim=0):
    return lax.dot_general(
        left, right, (((left_dim,), (right_dim,)), ((), ())), preferred_element_type=full_type
    )


def at_rows(start, count):
    return pl.ds(pl.multiple_of(start, 16), count)


def lanes(index, count):
    return pl.ds(pl.multiple_of(index * count, count), count)


def repeat(count, body):
    def step(index, carry):
        body(index)
        return carry

    lax.fori_loop(0, count, step, 0)


class Gather:
    def __init__(self, place, all_ref, half, send, recv, twin_recv):
        self.place, self.all, self.half = place, all_ref, half
        self.size = all_ref.shape[1] // (2 * GROUP)
        self.send, self.recv, self.twin_recv = send, recv, twin_recv
        self.p, self.q, self.p_next, self.q_next = place.axes(half == 1)
        self.own = self.block(self.q, self.p, place.z)
        self.sends = []
        z = place.z
        far = z // 2
        self.z_from = (z, 1 - z + 4 * far, 2 - far, 3 - 3 * far)
        inward, outward = 1 + lax.rem(z, 2), lax.rem(3 * z - 3 + 12, 12)
        self.inward, self.outward = place.at(place.x, place.y, inward), place.at(place.x, place.y, outward)
        across = place.at(place.x, place.y, 3 - z)
        self.z_next = (None, across, self.outward, self.outward)
        self.between = lax.rem(z, 3) != 0

    def block(self, q, p, z):
        return (q * 2 + p) * 4 + z

    def rows(self, block):
        return at_rows((self.half * GROUP + block) * self.size, self.size)

    def ref(self, block, kind):
        return self.all.at[kind, self.rows(block)]

    def pass_on(self, block, device, only=None):
        slot = len(self.sends)

        def copy():
            ref = self.ref(block, self.place.head)
            return remote(ref, ref, self.send.at[self.half, slot], self.recv.at[self.half, block], device)

        self.sends.append((copy, only))
        if only is None:
            copy().start()
        else:
            pl.when(only)(lambda: copy().start())

    def to_twin(self, block):
        slot = len(self.sends)

        def copy():
            ref = self.ref(block, self.place.head)
            return remote(ref, ref, self.send.at[self.half, slot], self.twin_recv.at[self.half, block], self.place.twin)

        self.sends.append((copy, None))
        copy().start()

    def landed(self, block):
        ref = self.ref(block, self.place.head)
        remote(ref, ref, self.send.at[self.half, 0], self.recv.at[self.half, block], self.p_next).wait_recv()

    def start(self):
        self.sends.clear()
        self.pass_on(self.own, self.inward)
        self.pass_on(self.own, self.outward, self.between)
        self.pass_on(self.own, self.p_next)

    def plane(self, side, other):
        q = self.q if side == 0 else 1 - self.q
        p = self.p if other == 0 else 1 - self.p
        return at_rows((self.half * GROUP + self.block(q, p, 0)) * self.size, 4 * self.size)

    def plane_copy(self, side, other, kind, slot, recv, device):
        ref = self.all.at[kind, self.plane(side, other)]
        return remote(ref, ref, self.send.at[self.half, slot], recv.at[self.half, GROUP + side * 2 + other], device)

    def plane_on(self, side, other, recv, device, lands=None):
        slot = len(self.sends)
        ref = self.all.at[self.place.head, self.plane(side, other)]
        side, other = (side, other) if lands is None else lands

        def copy():
            there = recv.at[self.half, GROUP + side * 2 + other]
            return remote(ref, ref, self.send.at[self.half, slot], there, device)

        self.sends.append((copy, None))
        copy().start()

    def forward(self, step):
        block = self.block(self.q, self.p, self.z_from[step])
        pl.when(self.between)(lambda: self.landed(block))
        self.pass_on(block, self.z_next[step], self.between)

    def z_step(self, step):
        block = self.block(self.q, self.p, self.z_from[step])
        pl.when(jnp.logical_not(self.between))(lambda: self.landed(block))
        self.pass_on(block, self.p_next)
        self.to_twin(block)
        if step == 3:
            self.plane_on(0, 0, self.recv, self.q_next, (1, 0))

    def p_step(self):
        for step in range(4):
            self.landed(self.block(self.q, 1 - self.p, self.z_from[step]))
        self.plane_on(0, 1, self.recv, self.q_next, (1, 1))
        self.plane_on(0, 1, self.twin_recv, self.place.twin)

    def q_step(self, other):
        self.plane_copy(1, other, self.place.head, 0, self.recv, self.q_next).wait_recv()
        self.plane_on(1, other, self.twin_recv, self.place.twin)

    def plane_landed(self, side, other):
        kind = 1 - self.place.head
        if side + other > 0:
            self.plane_copy(side, other, kind, 0, self.twin_recv, self.place.twin).wait_recv()
            return
        for step in range(1, 4):
            block = self.block(self.q, self.p, self.z_from[step])
            ref = self.ref(block, kind)
            remote(
                ref, ref, self.send.at[self.half, 0], self.twin_recv.at[self.half, block], self.place.twin
            ).wait_recv()

    def finish(self):
        for copy, only in self.sends:
            if only is None:
                copy().wait_send()
            else:
                pl.when(only)(lambda copy=copy: copy().wait_send())


def layer_kernel(
    tokens_any, query_any, key_any, value_any, out_any, inner_any, outer_any,
    memory_ref, index_ref, cot_ref, query_bias_ref, value_bias_ref, out_bias_ref, first_gain_ref, first_shift_ref,
    inner_bias_ref, outer_bias_ref, second_gain_ref, second_shift_ref,
    layer_any, memory_out_any, tokens_grad_any, memory_grad_any, sum_any, outer_grad_any, inner_grad_any, vec_any,
    rows, wq, wkv, wo, wi, wu, load_sem,
    pick, keys, values, pair_values, rows_m, query_m, probs, context_m, swap_out, swap_in,
    first_scaled, fig, slope, query_grad, kv_grad, spread, stage,
    all_ref, small_all, grads, inbox,
    part_t, got_t, query_d, context_d, normed_d, pool,
    g_send, g_recv, t_recv, r_send, r_recv, s_send, s_recv, x_send, x_recv,
    layer_out_ref, memory_out_ref, tokens_grad_ref, memory_grad_ref, sum_ref, outer_grad_ref, inner_grad_ref,
    vec_out_ref, store_sem,
):
    segs, seq, width = tokens_any.shape
    mem_len = memory_ref.shape[0]
    mem_pad = -(-mem_len // 32) * 32
    tall = seq + mem_pad
    masked = cot_ref.shape[1]
    m_rows = segs * masked
    own_seq = seq // 2
    own = own_seq + mem_pad
    half = query_any.shape[1]
    pairs = half // 128
    key_rows = keys.shape[1]
    hidden = inner_any.shape[1]
    place = Place()
    head = place.head
    gate = lax.broadcasted_iota(jnp.int32, (1, 128), 1) < HDIM
    score_scale = 1.0 / math.sqrt(HDIM)

    loads = []

    def load(src, dst):
        copy = pltpu.make_async_copy(src, dst, load_sem.at[len(loads)])
        copy.start()
        loads.append(copy)
        return copy

    stores = []

    def store(src, dst):
        copy = pltpu.make_async_copy(src, dst, store_sem.at[len(stores)])
        copy.start()
        stores.append(copy)

    load_rows = []
    for s in range(segs):
        load_rows.append(load(tokens_any.at[s], rows.at[pl.ds(s * tall, seq)]))
    load_kv = [load(key_any, wkv.at[:, pl.ds(0, half)]), load(value_any, wkv.at[:, pl.ds(half, half)])]
    load_q, load_o = load(query_any, wq), load(out_any, wo)
    load_i, load_u = load(inner_any, wi), load(outer_any, wu)

    barrier = pltpu.get_barrier_semaphore()
    partners = place.partners()
    for partner in partners:
        pl.semaphore_signal(barrier, inc=1, device_id=partner, device_id_type=MESH)

    def vector(ref, start=0, count=None):
        count = ref.shape[0] if count is None else count
        return ref[pl.ds(start, count)].astype(full_type).reshape(1, count)

    out_bias, first_gain, first_shift = vector(out_bias_ref), vector(first_gain_ref), vector(first_shift_ref)
    outer_bias, second_gain, second_shift = vector(outer_bias_ref), vector(second_gain_ref), vector(second_shift_ref)
    query_bias, value_bias = vector(query_bias_ref), vector(value_bias_ref)
    key_index = lax.broadcasted_iota(jnp.int32, (1, key_rows - seq), 1)
    key_mask = jnp.where(key_index < mem_len, 0.0, -1e30).astype(full_type)

    def inner_bias(part):
        return vector(inner_bias_ref, part * width, width)

    memory = memory_ref[...].astype(full_type)
    blank = jnp.zeros((mem_pad - mem_len, width), full_type)
    for s in range(segs):
        filled = jnp.concatenate([memory[:, s, :], blank], axis=0)
        rows[pl.ds(s * tall + seq, mem_pad)] = filled.astype(low_type)
    keys[:, pl.ds(tall, key_rows - tall)] = jnp.zeros((segs, key_rows - tall, half), low_type)
    values[:, pl.ds(tall, key_rows - tall)] = jnp.zeros((segs, key_rows - tall, half), low_type)
    for s in range(segs):
        hot = index_ref[s : s + 1] == lax.broadcasted_iota(jnp.int32, (seq, masked), 0)
        pick[s] = jnp.where(hot, 1.0, 0.0).astype(low_type)

    for copy in load_rows + load_kv:
        copy.wait()

    def key_value(s):
        both = dots(rows[at_rows(s * tall, tall)], wkv[...])
        keys[s, 0:tall] = both[:, :half].astype(low_type)
        values[s, 0:tall] = (both[:, half:] + value_bias).astype(low_type)

    repeat(segs, key_value)

    load_q.wait()
    for s in range(segs):
        m = pl.ds(s * masked, masked)
        found = dots(pick[s], rows[pl.ds(s * tall, seq)], 0, 0).astype(low_type)
        rows_m[m] = found
    query_m[...] = (dots(rows_m[...], wq[...]) + query_bias).astype(low_type)

    def apart(pair):
        zero = jnp.zeros_like(pair)
        return jnp.concatenate([jnp.where(gate, pair, zero), jnp.where(gate, zero, pair)], axis=0)

    def masked_attention(i):
        s, pair = i // pairs, lax.rem(i, pairs)
        m, cols = at_rows(s * masked, masked), lanes(pair, 128)
        scores = dots(apart(query_m[m, cols]), keys[s, :, cols], 1, 1) * score_scale
        scores = jnp.concatenate([scores[:, :seq], scores[:, seq:] + key_mask], axis=1)
        raised = jnp.exp(scores - jnp.max(scores, axis=1, keepdims=True))
        share = raised / jnp.sum(raised, axis=1, keepdims=True)
        probs[i] = share
        found = dots(share.astype(low_type), values[s, :, cols])
        context_m[m, cols] = jnp.where(gate, found[:masked], found[masked:]).astype(low_type)

    repeat(segs * pairs, masked_attention)

    exchanges = []

    def twin_copy(src, dst):
        slot = len(exchanges)
        copy = remote(src, dst, x_send.at[slot], x_recv.at[slot], place.twin)
        copy.start()
        exchanges.append(copy)
        return copy

    def swap(slot, partial):
        swap_out[slot] = partial.astype(low_type)
        return twin_copy(swap_out.at[slot], swap_in.at[slot])

    def swapped(slot, copy):
        copy.wait_recv()
        return swap_out[slot].astype(full_type) + swap_in[slot].astype(full_type)

    load_o.wait()
    partial = dots(context_m[...], wo[...])
    pl.semaphore_wait(barrier, len(partners))
    swapping = swap(0, partial)

    def spread_values(i):
        s, pair = i // pairs, lax.rem(i, pairs)
        v = values[s, :, lanes(pair, 128)]
        ones = jnp.ones_like(v)
        pair_values[i, 0] = jnp.where(gate, v, ones)
        pair_values[i, 1] = jnp.where(gate, ones, v)

    repeat(segs * pairs, spread_values)

    load_i.wait()
    load_u.wait()
    scaled, inverse = norm_stats(rows_m[...].astype(full_type) + (swapped(0, swapping) + out_bias))
    first_scaled[...] = scaled
    normed = scaled * first_gain + first_shift
    normed_low = normed.astype(low_type)
    gathers = [Gather(place, all_ref, part, g_send, g_recv, t_recv) for part in range(2)]
    for part, gather in enumerate(gathers):
        all_ref[0, gather.rows(gather.own)] = normed_low[part * masked : (part + 1) * masked]
    @pl.when(head == 0)
    def _():
        for gather in gathers:
            gather.start()

    partial = jnp.zeros((m_rows, width), full_type)
    parts = hidden // width
    for part in range(parts):
        cols = slice(part * width, (part + 1) * width)
        pre_act = dots(normed_low, wi[:, cols]) + inner_bias(part)
        share = 0.5 * (1.0 + lax.erf(pre_act * root_half))
        slope[:, cols] = share + pre_act * jnp.exp(-0.5 * pre_act * pre_act) * gauss_norm
        partial += dots((pre_act * share).astype(low_type), wu[cols])
    swapping = swap(1, partial)
    scaled2, inverse2 = norm_stats(normed + (swapped(1, swapping) + outer_bias))
    upstream = cot_ref[...].reshape(m_rows, width).astype(full_type)
    second_in_grad = norm_backward(upstream, scaled2, inverse2, second_gain)
    outer_grad = second_in_grad.astype(low_type)
    for part, gather in enumerate(gathers):
        all_ref[1, gather.rows(gather.own)] = outer_grad[part * masked : (part + 1) * masked]

    @pl.when(head == 1)
    def _():
        for gather in gathers:
            gather.start()

    small = SmallGather(place, small_all, s_send, s_recv)
    mine = small.line + place.z
    reduces = [
        Reduce(place, slot, grads.at[slot], sum_ref.at[slot], inbox.at[slot], r_send, r_recv) for slot in range(4)
    ]

    def tick(name):
        for event in PLAN.get(name, ()):
            if event[0] == "r":
                reduces[int(event[1])].step(int(event[2]))
            elif event[0] == "s":
                getattr(small, "step_" + event[1])()
            else:
                for gather in gathers:
                    if event[0] == "F":
                        gather.forward(int(event[1]))
                    elif event[0] == "z":
                        gather.z_step(int(event[1]))
                    elif event[0] == "p":
                        gather.p_step()
                    else:
                        gather.q_step(int(event[1]))

    def column_sum(value):
        return jnp.sum(value, axis=0, keepdims=True)

    second_gain_part, second_shift_part = column_sum(upstream * scaled2), column_sum(upstream)

    partial = jnp.zeros((m_rows, width), full_type)
    for part in range(parts):
        cols = slice(part * width, (part + 1) * width)
        inner_grad = (dots(outer_grad, wu[cols], 1, 1) * slope[:, cols]).astype(low_type)
        partial += dots(inner_grad, wi[:, cols], 1, 1)
    swapping = swap(2, partial)
    tick("swap")
    normed_grad = second_in_grad + swapped(2, swapping)
    scaled = first_scaled[...]
    first_in_grad = norm_backward(normed_grad, scaled, inverse, first_gain)
    fig[...] = first_in_grad
    attention_grad = first_in_grad.astype(low_type)
    small_all[mine, 0:1] = column_sum(attention_grad.astype(full_type))
    small_all[mine, 1:2] = column_sum(normed_grad * scaled)
    small_all[mine, 2:3] = column_sum(normed_grad)
    small_all[mine, 3:4] = second_gain_part
    small_all[mine, 4:5] = second_shift_part
    out_grad = dots(context_m[...], attention_grad, 0, 0).astype(low_type)
    grads[0, 0:half] = out_grad[:, :half]
    grads[0, half : 2 * half] = out_grad[:, half:]
    reduces[0].step(1)
    stage[...] = dots(attention_grad, wo[...], 1, 1).astype(low_type)

    def masked_back(i):
        s, pair = i // pairs, lax.rem(i, pairs)
        m, cols = at_rows(s * masked, masked), lanes(pair, 128)
        value_cols = pl.ds(pl.multiple_of(half + pair * 128, 128), 128)
        context_grad = apart(stage[m, cols])
        share = probs[i]
        weighed = share * dots(context_grad, values[s, :, cols], 1, 1)
        score_grad = (weighed - share * jnp.sum(weighed, axis=1, keepdims=True)).astype(low_type)
        all_rows = at_rows(s * tall, tall)
        found = dots(share.astype(low_type), context_grad, 0, 0)
        kv_grad[all_rows, value_cols] = found[:tall].astype(low_type)
        found = dots(score_grad, apart(query_m[m, cols]), 0, 0) * score_scale
        kv_grad[all_rows, cols] = found[:tall].astype(low_type)
        found = dots(score_grad, keys[s, :, cols]) * score_scale
        query_grad[m, cols] = jnp.where(gate, found[:masked], found[masked:]).astype(low_type)

    repeat(segs * pairs, masked_back)
    tick("back")
    grads[1] = dots(rows_m[...], query_grad[...], 0, 0).astype(low_type)
    small_all[mine, 5:6] = jnp.concatenate(
        [
            column_sum(query_grad[...].astype(full_type)),
            column_sum(kv_grad[:, half:].astype(full_type)),
        ],
        axis=1,
    )
    small_all[mine, 6:8] = jnp.zeros((2, width), full_type)
    tick("query")

    def key_value_grad(c):
        cols = lanes(c, 256)
        found = dots(rows[:, cols], kv_grad[...], 0, 0).astype(low_type)
        grads[2, cols] = found[:, :half]
        grads[3, cols] = found[:, half:]

    repeat(width // 256, key_value_grad)
    reduces[2].step(1)
    reduces[3].step(1)
    tick("kv")

    masked_part = dots(query_grad[...], wq[...], 1, 1) + jnp.where(head == 0, fig[...], 0.0)
    high = masked_part.astype(low_type)
    rest = (masked_part - high.astype(full_type)).astype(low_type)
    for s in range(segs):
        spread[s, 0:masked] = high[s * masked : (s + 1) * masked]
        spread[s, masked : 2 * masked] = rest[s * masked : (s + 1) * masked]

    def row_grad(i):
        s, c = i // 2, lax.rem(i, 2)
        here = at_rows(s * tall + c * own_seq, own_seq)
        found = dots(kv_grad[here], wkv[...], 1, 1)
        chosen = pick[s, at_rows(c * own_seq, own_seq)]
        found += dots(chosen, spread[s, 0:masked]) + dots(chosen, spread[s, masked : 2 * masked])
        part_t[here] = found.astype(low_type)

    repeat(segs, row_grad)
    tick("rows0")
    repeat(segs, lambda i: row_grad(i + segs))
    for s in range(segs):
        here = pl.ds(s * tall + seq, mem_pad)
        part_t[here] = dots(kv_grad[here], wkv[...], 1, 1).astype(low_type)

    def send_rows(source, target, s):
        away = at_rows(s * tall + (1 - head) * own_seq, own_seq)
        one = twin_copy(source.at[away], target.at[pl.ds(s * own, own_seq)])
        two = twin_copy(source.at[pl.ds(s * tall + seq, mem_pad)], target.at[pl.ds(s * own + own_seq, mem_pad)])
        return one, two

    moved_t = [send_rows(part_t, got_t, s) for s in range(segs)]
    tick("rows1")
    reduces[1].step(1)

    pool_at = 0

    def region(count):
        nonlocal pool_at
        pool_at += count
        return pool.at[pl.ds(pool_at - count, count)]

    part_a, got_a, low_d = region(segs * tall), region(segs * own), region(segs * tall)
    part_f, got_f = region(segs * tall), region(segs * own)
    active = region(parts * tall)

    def dense_query(s):
        here = at_rows(s * tall, tall)
        query_d[here] = (dots(rows[here], wq[...]) + query_bias).astype(low_type)

    repeat(segs, dense_query)
    exp_scale = score_scale * math.log2(math.e)

    def dense_attention(s, pair):
        cols = lanes(pair, 128)
        block_rows = tall // 2
        k = keys[s, :, cols]
        for block in range(2):
            here = at_rows(s * tall + block * block_rows, block_rows)
            query = query_d[here, cols]
            zero = jnp.zeros_like(query)
            found = []
            for side in range(2):
                lone = jnp.where(gate, query, zero) if side == 0 else jnp.where(gate, zero, query)
                scores = dots(lone, k, 1, 1)
                scores = jnp.concatenate([scores[:, :seq], scores[:, seq:] + key_mask], axis=1)
                raised = jnp.exp2((scores - jnp.max(scores, axis=1, keepdims=True)) * exp_scale)
                found.append(dots(raised.astype(low_type), pair_values[s * pairs + pair, side]))
            top = jnp.where(gate, found[0], found[1])
            total = pltpu.roll(jnp.where(gate, found[1], found[0]), HDIM, 1)
            context_d[here, cols] = (top / total).astype(low_type)

    def dense_out(s):
        here = pl.ds(s * tall, tall)
        part_a[here] = dots(context_d[here], wo[...]).astype(low_type)

    def norm_first(s, local, count):
        tokens_here = at_rows(s * tall + head * own_seq + local, count)
        here = pl.ds(s * tall + seq, count) if local == own_seq else tokens_here
        near = pl.ds(s * own + local, count)
        total = part_a[here].astype(full_type) + got_a[near].astype(full_type) + out_bias
        scaled, _ = norm_stats(rows[here].astype(full_type) + total)
        value = scaled * first_gain + first_shift
        normed_d[near] = value
        low_d[here] = value.astype(low_type)

    def norm_second(s, local, count):
        tokens_here = at_rows(s * tall + head * own_seq + local, count)
        here = pl.ds(s * tall + seq, count) if local == own_seq else tokens_here
        near = pl.ds(s * own + local, count)
        total = part_f[here].astype(full_type) + got_f[near].astype(full_type) + outer_bias
        scaled, _ = norm_stats(normed_d[near] + total)
        value = (scaled * second_gain + second_shift).astype(low_type)
        if local == own_seq:
            memory_out_ref[s] = value
        else:
            layer_out_ref[s, pl.ds(local, count)] = value

    chunk = 128
    spans = [(c * chunk, chunk) for c in range(own_seq // chunk)] + [(own_seq, mem_pad)]
    moved_a = []
    for s in range(segs):
        for pair in range(pairs):
            dense_attention(s, pair)
            tick("pair%d" % (s * pairs + pair))
        dense_out(s)
        moved_a.append(send_rows(part_a, got_a, s))
        tick("out%d" % s)
    moved_n = []
    for s in range(segs):
        for copy in moved_a[s]:
            copy.wait_recv()
        for local, count in spans:
            norm_first(s, local, count)
        ours = low_d.at[at_rows(s * tall + head * own_seq, own_seq)]
        moved_n.append(twin_copy(ours, ours))
        tick("norm%d" % s)
    for s in range(segs):
        for copy in moved_t[s]:
            copy.wait_recv()
        ours = at_rows(s * tall + head * own_seq, own_seq)
        near = got_t[pl.ds(s * own, own_seq)].astype(full_type)
        tokens_grad_ref[s] = (part_t[ours].astype(full_type) + near).astype(low_type)
        near = got_t[pl.ds(s * own + own_seq, mem_pad)].astype(full_type)
        memory_grad_ref[s] = (part_t[pl.ds(s * tall + seq, mem_pad)].astype(full_type) + near).astype(low_type)
    store(tokens_grad_ref, tokens_grad_any)
    store(memory_grad_ref, memory_grad_any)
    moved_f = []
    for s in range(segs):
        moved_n[s].wait_recv()
        here = pl.ds(s * tall, tall)
        for part in range(parts):
            cols = slice(part * width, (part + 1) * width)
            pre_act = dots(low_d[here], wi[:, cols]) + inner_bias(part)
            active[pl.ds(part * tall, tall)] = (0.5 * pre_act * (1.0 + lax.erf(pre_act * root_half))).astype(low_type)
            tick("ff%d%d" % (s, part))
        partial = dots(active[pl.ds(0, tall)], wu[0:width])
        for part in range(1, parts):
            partial += dots(active[pl.ds(part * tall, tall)], wu[part * width : (part + 1) * width])
        part_f[here] = partial.astype(low_type)
        moved_f.append(send_rows(part_f, got_f, s))
        tick("ff%d2" % s)
    for s in range(segs):
        for copy in moved_f[s]:
            copy.wait_recv()
        for local, count in spans:
            norm_second(s, local, count)
        tick("last%d" % s)
    store(layer_out_ref, layer_any)
    store(memory_out_ref, memory_out_any)
    for copy in exchanges:
        copy.wait_send()

    total_rows = all_ref.shape[1]
    active_all, inner_grad_all = pool.at[pl.ds(0, total_rows)], pool.at[pl.ds(total_rows, total_rows)]
    ones = jnp.ones((16, total_rows), low_type)

    def hidden_block(part, here):
        cols = slice(part * width, (part + 1) * width)
        pre_act = dots(all_ref[0, here], wi[:, cols]) + inner_bias(part)
        back = dots(all_ref[1, here], wu[cols], 1, 1)
        share = 0.5 * (1.0 + lax.erf(pre_act * root_half))
        active_all[here] = (pre_act * share).astype(low_type)
        bell = pre_act * jnp.exp(-0.5 * pre_act * pre_act) * gauss_norm
        inner_grad_all[here] = (back * (share + bell)).astype(low_type)

    blocks = 4
    block_rows = total_rows // blocks
    for part in range(parts):
        cols = slice(part * width, (part + 1) * width)
        if part == 0:
            for group, (side, other) in enumerate(((0, 0), (0, 1), (1, 0), (1, 1))):
                tick("to%d" % group)
                for gather in gathers:
                    gather.plane_landed(side, other)
                starts = [gather.plane(side, other).start for gather in gathers]

                def both_halves(i):
                    start = starts[0] * (1 - i) + starts[1] * i
                    hidden_block(0, at_rows(start, total_rows // 8))

                repeat(2, both_halves)
                tick("mid%d" % group)
        else:
            repeat(blocks // 2, lambda i: hidden_block(part, at_rows(i * block_rows, block_rows)))
            tick("half%d" % part)
            repeat(blocks // 2, lambda i: hidden_block(part, at_rows((i + blocks // 2) * block_rows, block_rows)))
            tick("wide%d" % (3 * part - 1))
        outer_grad_ref[cols] = dots(active_all[...], all_ref[1], 0, 0).astype(low_type)
        store(outer_grad_ref.at[cols], outer_grad_any.at[cols])
        tick("wide%d" % (3 * part))
        inner_grad_ref[:, cols] = dots(all_ref[0], inner_grad_all[...], 0, 0).astype(low_type)
        store(inner_grad_ref.at[:, cols], inner_grad_any.at[:, cols])
        vec_out_ref[8 + part : 9 + part] = dots(ones, inner_grad_all[...])[0:1]
        tick("wide%d" % (3 * part + 1))
    vec_out_ref[10:11] = dots(ones, all_ref[1])[0:1]
    small.finish()
    total = small_all[0]
    for block in range(1, GROUP):
        total += small_all[block]
    vec_out_ref[0:8] = total
    vec_out_ref[11:16] = jnp.zeros((5, width), full_type)
    store(vec_out_ref, vec_any)
    for slot, reduce in enumerate(reduces):
        reduce.finish()
        store(sum_ref.at[slot], sum_any.at[slot])
    for gather in gathers:
        gather.finish()
    for copy in stores:
        copy.wait()


def layer(tokens, memory, weights, index, cotangent, vectors):
    segs, seq, width = tokens.shape
    mem_pad, masked = -(-memory.shape[0] // 32) * 32, cotangent.shape[1]
    half, hidden = weights[0].shape[1], weights[4].shape[1]
    tall, own, m_rows = seq + mem_pad, seq // 2 + mem_pad, segs * masked
    key_rows = -(-tall // 128) * 128
    pairs, parts = half // 128, hidden // width
    total_rows = GROUP * m_rows
    pool_rows = max(2 * total_rows, (3 * segs + parts) * tall + 2 * segs * own)
    vmem, anywhere = pl.BlockSpec(memory_space=pltpu.VMEM), pl.BlockSpec(memory_space=pl.ANY)

    def low(*shape):
        return pltpu.VMEM(shape, low_type)

    def full(*shape):
        return pltpu.VMEM(shape, full_type)

    def result(*shape):
        return jax.ShapeDtypeStruct(shape, low_type)

    sems = pltpu.SemaphoreType.DMA
    return pl.pallas_call(
        layer_kernel,
        out_shape=(
            result(segs, seq // 2, width),
            result(segs, mem_pad, width),
            result(segs, seq // 2, width),
            result(segs, mem_pad, width),
            result(4, width, half),
            result(hidden, width),
            result(width, hidden),
            jax.ShapeDtypeStruct((16, width), full_type),
        ),
        in_specs=[anywhere] * 7 + [vmem] * (3 + len(vectors)),
        out_specs=(anywhere,) * 8,
        scratch_shapes=[
            low(segs * tall, width), low(width, half), low(width, 2 * half), low(half, width),
            low(width, hidden), low(hidden, width), sems((segs + 6,)),
            low(segs, seq, masked), low(segs, key_rows, half), low(segs, key_rows, half),
            low(segs * pairs, 2, key_rows, 128), low(m_rows, width), low(m_rows, half),
            full(segs * pairs, 2 * masked, key_rows), low(m_rows, half), low(3, m_rows, width), low(3, m_rows, width),
            full(m_rows, width), full(m_rows, width), full(m_rows, hidden), low(m_rows, half),
            low(segs * tall, 2 * half), low(segs, 2 * masked, width), low(m_rows, half),
            low(2, total_rows, width), full(GROUP, 8, width), low(4, width, half),
            low(4, width - width // GROUP, half),
            low(segs * tall, width), low(segs * own, width), low(segs * tall, half), low(segs * tall, half),
            full(segs * own, width), low(pool_rows, width),
            sems((2, 24)), sems((2, 20)), sems((2, 20)), sems((4, 10)), sems((4, 10)),
            sems((5,)), sems((5,)), sems((3 + 7 * segs,)), sems((3 + 7 * segs,)),
            low(segs, seq // 2, width), low(segs, mem_pad, width), low(segs, seq // 2, width), low(segs, mem_pad, width),
            low(4, width, half), low(hidden, width), low(width, hidden), full(16, width), sems((9 + 2 * parts,)),
        ],
        compiler_params=pltpu.CompilerParams(
            collective_id=0, has_side_effects=True, vmem_limit_bytes=63 * 2**20
        ),
    )(tokens, *weights, memory, index, cotangent, *vectors)


def result_kernel(
    layer_in, memory_in, tokens_in, memory_grad_in, out_a, out_b, query_in, key_in, value_in, outer_in, inner_in, vecs,
    layer_out, memory_out, tokens_grad, memory_grad, query_grad, query_bias, key_grad, value_grad, value_bias,
    out_grad, out_bias, first_gain, first_shift, inner_grad, inner_bias, outer_grad, outer_bias, second_gain, second_shift,
):
    layer_out[...] = layer_in[...]
    tokens_grad[...] = tokens_in[...]
    half = query_grad.shape[1]
    out_grad[:, :half] = out_a[0].astype(full_type)
    out_grad[:, half:] = out_b[0].astype(full_type)
    query_grad[...] = query_in[0].astype(full_type)
    key_grad[...] = key_in[0].astype(full_type)
    value_grad[...] = value_in[0].astype(full_type)
    inner_grad[...] = inner_in[...].astype(full_type)
    outer_grad[...] = outer_in[...].astype(full_type)

    @pl.when(pl.program_id(0) == 0)
    def _():
        count = memory_out.shape[0]
        upper = lax.axis_index("head") > 0
        for source, target in ((memory_in, memory_out), (memory_grad_in, memory_grad)):
            for s in range(source.shape[0]):
                value = source[s].astype(full_type)
                target[:, s] = jnp.where(upper, value[count : 2 * count], value[:count]).astype(low_type)
        for row, target in enumerate((out_bias, first_gain, first_shift, second_gain, second_shift)):
            target[...] = vecs[row]
        query_bias[...] = vecs[5, :half]
        value_bias[...] = vecs[5, half:]
        width = vecs.shape[1]
        for part in range(inner_bias.shape[0] // width):
            inner_bias[pl.ds(part * width, width)] = vecs[8 + part]
        outer_bias[...] = vecs[10]


def results(layer_out, memory_out, tokens_grad, memory_grad, sums, outer_grad, inner_grad, vecs, own_mem):
    segs, own_seq, width = layer_out.shape
    hidden, half = outer_grad.shape[0], sums.shape[2]
    steps = 4

    def rows_of(shape, dim):
        block = tuple(size // steps if i == dim else size for i, size in enumerate(shape))
        return pl.BlockSpec(block, lambda i: tuple(i if d == dim else 0 for d in range(len(shape))))

    def whole(*shape):
        return pl.BlockSpec(shape, lambda i: (0,) * len(shape))

    def part_of_sums(slot, rows, offset=0):
        return pl.BlockSpec((1, rows, half), lambda i: (slot, i + offset, 0))

    def full(*shape):
        return jax.ShapeDtypeStruct(shape, full_type)

    out_rows = half // steps
    moved = rows_of(layer_out.shape, 1)
    memory_shape = (own_mem, segs, width)
    square, tall, wide, out = (width, half), (hidden, width), (width, hidden), (half, width)
    shapes = (
        jax.ShapeDtypeStruct(layer_out.shape, low_type),
        jax.ShapeDtypeStruct(memory_shape, low_type),
        jax.ShapeDtypeStruct(layer_out.shape, low_type),
        jax.ShapeDtypeStruct(memory_shape, low_type),
        full(*square), full(half), full(*square), full(*square), full(half), full(*out), full(width), full(width),
        full(width), full(*wide), full(hidden), full(*tall), full(width), full(width), full(width),
    )
    specs = tuple(
        moved if i in (0, 2) else rows_of(shape.shape, 0) if len(shape.shape) == 2 else whole(*shape.shape)
        for i, shape in enumerate(shapes)
    )
    return pl.pallas_call(
        result_kernel,
        grid=(steps,),
        out_shape=shapes,
        in_specs=[
            moved, whole(*memory_out.shape), moved, whole(*memory_out.shape),
            part_of_sums(0, out_rows), part_of_sums(0, out_rows, steps),
            part_of_sums(1, width // steps), part_of_sums(2, width // steps), part_of_sums(3, width // steps),
            rows_of(tall, 0), rows_of(wide, 0), whole(*vecs.shape),
        ],
        out_specs=specs,
        compiler_params=pltpu.CompilerParams(vmem_limit_bytes=63 * 2**20),
    )(
        layer_out, memory_out, tokens_grad, memory_grad, sums, sums, sums, sums, sums, outer_grad, inner_grad, vecs
    )


def across_groups(values):
    size = lax.axis_size("dp")
    if size == GROUP:
        return values
    total = moved = values.astype(full_type)
    for _ in range(size // GROUP - 1):
        moved = lax.ppermute(moved, "dp", [(i, (i + GROUP) % size) for i in range(size)])
        total = total + moved
    return total


def on_device(
    tokens,
    memory,
    query_weight,
    query_bias,
    key_weight,
    value_weight,
    value_bias,
    out_weight,
    out_bias,
    first_gain,
    first_shift,
    inner_weight,
    inner_bias,
    outer_weight,
    outer_bias,
    second_gain,
    second_shift,
    masked_rows,
    cotangent,
):
    vectors = (
        query_bias, value_bias, out_bias, first_gain, first_shift, inner_bias, outer_bias, second_gain, second_shift,
    )
    weights = (query_weight, key_weight, value_weight, out_weight, inner_weight, outer_weight)
    rows = layer(tokens, jnp.swapaxes(memory, 0, 1), weights, masked_rows, cotangent, vectors)
    sums = tuple(across_groups(values) for values in rows[4:])
    outputs = list(results(*rows[:4], *sums, memory.shape[1] // 2))
    outputs[1], outputs[3] = jnp.swapaxes(outputs[1], 0, 1), jnp.swapaxes(outputs[3], 0, 1)
    return tuple(outputs)


def solution(mesh):
    return jax.shard_map(
        on_device,
        mesh=mesh,
        in_specs=(
            P("dp", None, None),
            P("dp", None, None),
            P(None, "head"),
            P("head"),
            P(None, "head"),
            P(None, "head"),
            P("head"),
            P("head", None),
            P(),
            P(),
            P(),
            P(None, "head"),
            P("head"),
            P("head", None),
            P(),
            P(),
            P(),
            P("dp", None),
            P("dp", None, None),
        ),
        out_specs=(
            P("dp", "head", None),
            P("dp", "head", None),
            P("dp", "head", None),
            P("dp", "head", None),
            P(None, "head"),
            P("head"),
            P(None, "head"),
            P(None, "head"),
            P("head"),
            P("head", None),
            P(),
            P(),
            P(),
            P(None, "head"),
            P("head"),
            P("head", None),
            P(),
            P(),
            P(),
        ),
        check_vma=False,
    )
```
